256 devices in a mesh: ctx: 32 (over z, y), head: 4 (over x), side: 2 (over core).
Axes of the slice: x: 4, y: 4, z: 8, core: 2. Of those that a mesh axis runs over, the one named last changes fastest.
Arguments:
- x_in: bfloat16 [2, 16384, 8192], P('side', 'ctx', 'head'), may hold values from -6 to 6
- bc_in: bfloat16 [2, 16384, 2, 1024], P('side', 'ctx', None, 'head'), may hold values from -6 to 6
- z_in: bfloat16 [2, 16384, 8192], P('side', 'ctx', 'head'), may hold values from -6 to 6
- dt_in: float32 [2, 16384, 128], P('side', 'ctx', 'head'), may hold values from -4 to 11
- conv_x_w: float32 [4, 8192], P(None, 'head'), may hold values from -3 to 3
- conv_x_b: float32 [8192], P('head'), may hold values from -1 to 0
- conv_bc_w: float32 [4, 2, 1024], P(None, None, 'head'), may hold values from -3 to 3
- conv_bc_b: float32 [2, 1024], P(None, 'head'), may hold values from -1 to 0
- a_log: float32 [128], P('head'), may hold values from -5 to 2.7
- dt_bias: float32 [128], P('head'), may hold values from -7 to -2
- skip_d: float32 [128], P('head'), may hold values from 0.5 to 1.5
- norm_gain: float32 [8192], P('head'), may hold values from 0.5 to 1.5
- lengths: int32 [2, 32], P('side'), may hold values from 1 to 1024, as said below
- owner_slot: int32 [2, 32], P('side'), may hold values from 0 to 31, each once within a row
Outputs:
- mixed: bfloat16 [2, 16384, 8192], P('side', 'ctx', 'head')
- handed_state: float32 [2, 32, 128, 64, 128], P('side', 'ctx', 'head')
- handed_tail_x: bfloat16 [2, 32, 3, 8192], P('side', 'ctx', None, 'head')
- handed_tail_bc: bfloat16 [2, 32, 3, 2, 1024], P('side', 'ctx', None, None, 'head')
The draws below stay inside these ranges and needn't reach their ends.
Inputs may be any that keep to these rules, and one draw needn't show every extreme that they name: In each section the lengths add up to 16384. No block of 512 tokens that starts at a multiple of 512 holds the last token of more than 2 requests, and in each section some such block holds exactly 2. In each section some request holds exactly 1024 tokens.
All inputs are finite; a program needn't handle non-finite values.
Results may differ from the reference program's by a relative error of at most 0.0059.
Values may be sent and summed in bfloat16 or wider, within the bound.
No kernel may reach another device: no remote copies, remote signals or barrier semaphores. Data moves between devices by JAX's collectives and lax.ppermute only.
A program may use at most 128 MiB of HBM per device.

```python
import jax
import jax.numpy as jnp
from jax import lax

SCAN_LANE_COUNT = 128
HEAD_DIM = 64
STATE = 128
GROUPS = 8
KW = 4
STRETCH = 128
TOK_DEV = 512
DIN = 8192
GN = 1024
BATCH_POSITIONS = 16384
REQS = 32
ENDS = 2


def pick_spots(key):
    return jax.random.permutation(key, TOK_DEV - 1)[:ENDS].astype(jnp.int32)


def section_lengths(key):
    shard_total = BATCH_POSITIONS // TOK_DEV
    half_shard = TOK_DEV // 2
    gap_key, full_key, seed_for_location = jax.random.split(key, 3)
    gap_shard = jax.random.randint(gap_key, (), 1, shard_total - 1).astype(jnp.int32)
    drawn_full = ((gap_shard + 1 + jax.random.randint(full_key, (), 0, shard_total - 1)) % shard_total).astype(jnp.int32)
    full_shard = jnp.where(gap_shard + 1 == shard_total - 1, gap_shard + 1, drawn_full).astype(jnp.int32)
    spots = jax.vmap(pick_spots)(jax.random.split(seed_for_location, shard_total))
    lower = jnp.min(spots, axis=1)
    upper = jnp.max(spots, axis=1)
    shard = jnp.arange(shard_total, dtype=jnp.int32)
    is_last = shard == shard_total - 1
    before_gap = shard == gap_shard - 1
    after_gap = shard == gap_shard + 1
    is_full = shard == full_shard
    first_spot = jnp.where(before_gap, jnp.where(is_full, lower % (half_shard - 1), half_shard - 1), jnp.where(after_gap, half_shard - 1, jnp.where(is_last, jnp.where(is_full, lower, TOK_DEV - 1), lower))).astype(jnp.int32)
    second_spot = jnp.where(before_gap, half_shard - 1, jnp.where(after_gap, jnp.where(is_last, TOK_DEV - 1, half_shard + upper % (TOK_DEV - half_shard)), jnp.where(is_last, TOK_DEV - 1, upper))).astype(jnp.int32)
    sentinel = 2 * shard_total * TOK_DEV
    first_end = jnp.where(shard != gap_shard, shard * TOK_DEV + first_spot, sentinel)
    second_end = jnp.where(is_full, shard * TOK_DEV + second_spot, sentinel)
    last_token = jnp.sort(jnp.concatenate([first_end, second_end]).astype(jnp.int32))[:REQS]
    previous = jnp.concatenate([jnp.full((1,), -1, jnp.int32), last_token[:-1]])
    return (last_token - previous).astype(jnp.int32)


def draw_lengths(key, part):
    key = jax.random.fold_in(key, 3)
    return jnp.stack([section_lengths(jax.random.fold_in(key, 0)), section_lengths(jax.random.fold_in(key, 1))])


def draw_dt_in(key, part):
    key = jax.random.fold_in(key, 11)
    seed_for_background, seed_for_location, seed_for_spike = jax.random.split(key, 3)
    background_level = jnp.clip(0.7 * jax.random.normal(seed_for_background, (2, BATCH_POSITIONS, SCAN_LANE_COUNT), jnp.float32), -4.0, 4.0)
    spots = jax.random.randint(seed_for_location, (2, 4), 0, BATCH_POSITIONS)
    places = jnp.arange(BATCH_POSITIONS)
    perturbed_positions = jnp.any(places[None, :, None] == spots[:, None, :], axis=2)
    spike_magnitude = jax.random.uniform(seed_for_spike, (2, BATCH_POSITIONS, SCAN_LANE_COUNT), jnp.float32, 9.0, 11.0)
    return jnp.where(perturbed_positions[:, :, None], spike_magnitude, background_level).astype(jnp.float32)


def draw_dt_bias(key, part):
    key = jax.random.fold_in(key, 12)
    lower, upper = (-7.0, -2.0)
    return jax.random.uniform(key, (SCAN_LANE_COUNT,), jnp.float32, lower, upper)


def draw_a_log(key, part):
    key = jax.random.fold_in(key, 13)
    lower, upper = (-5.0, 2.7)
    return jax.random.uniform(key, (SCAN_LANE_COUNT,), jnp.float32, lower, upper)


def block_scale(rng, extent, cuts, least, top_value):
    factor_of, own = 1.0, jax.random.fold_in(rng, 6)
    for axis_at, blocks in cuts:
        steps = jnp.exp(jax.random.uniform(jax.random.fold_in(own, axis_at), (blocks,), jnp.float32, least / len(cuts), top_value / len(cuts)))
        factor_of = factor_of * jnp.repeat(steps, extent[axis_at] // blocks).reshape([-1 if axis == axis_at else 1 for axis in range(len(extent))])
    return factor_of


def noise(own_key, dims, width, limit, cuts=(), kind=jnp.bfloat16):
    level = block_scale(own_key, dims, cuts, -0.22, 0.18) if cuts else 1.0
    drawn = jax.random.normal(own_key, dims, jnp.float32) * width * level
    return jnp.minimum(jnp.maximum(drawn, -limit), limit).astype(kind)


def setup_inputs(seed: int = 0) -> dict:
    streams_of = jax.random.split(jax.random.key(seed), 15)
    return {
        "x_in": noise(streams_of[0], (2, BATCH_POSITIONS, DIN), 1.0, 6.0, ((0, 2), (1, 32), (2, 4))),
        "bc_in": noise(streams_of[1], (2, BATCH_POSITIONS, 2, GN), 1.0, 6.0, ((0, 2), (1, 32), (3, 4))),
        "z_in": noise(streams_of[2], (2, BATCH_POSITIONS, DIN), 1.0, 6.0, ((0, 2), (1, 32), (2, 4))),
        "dt_in": draw_dt_in(jax.random.fold_in(streams_of[14], 71), 0),
        "conv_x_w": noise(streams_of[4], (KW, DIN), KW ** -0.5, 3.0, ((1, 4),), jnp.float32),
        "conv_x_b": jnp.clip(-1.0 + 1.0 * jax.random.uniform(streams_of[5], (DIN,), jnp.float32) ** block_scale(streams_of[5], (DIN,), ((0, 4),), -0.2, 0.2), -1.0, 0.0),
        "conv_bc_w": noise(streams_of[6], (KW, 2, GN), KW ** -0.5, 3.0, ((2, 4),), jnp.float32),
        "conv_bc_b": jnp.clip(-1.0 + 1.0 * jax.random.uniform(streams_of[7], (2, GN), jnp.float32) ** block_scale(streams_of[7], (2, GN), ((1, 4),), -0.2, 0.2), -1.0, 0.0),
        "a_log": draw_a_log(jax.random.fold_in(streams_of[14], 71), 0),
        "dt_bias": draw_dt_bias(jax.random.fold_in(streams_of[14], 71), 0),
        "skip_d": jnp.clip(0.5 + 1.0 * jax.random.uniform(streams_of[10], (SCAN_LANE_COUNT,), jnp.float32) ** block_scale(streams_of[10], (SCAN_LANE_COUNT,), ((0, 4),), -0.2, 0.2), 0.5, 1.5),
        "norm_gain": jnp.clip(1.0 + 0.1 * jax.random.normal(streams_of[11], (DIN,), jnp.float32), 0.5, 1.5),
        "lengths": draw_lengths(jax.random.fold_in(streams_of[14], 71), 0),
        "owner_slot": jax.vmap(lambda own: jax.random.permutation(own, REQS))(jax.random.split(streams_of[13], 2)).reshape((2, REQS)).astype(jnp.int32),
    }


EPS = 1e-05

def conv_silu(padded, kernel, offset_bias, position, first_token):
    tap_count = kernel.shape[0]
    row_count = position.shape[0]
    summed = jnp.zeros((row_count, padded.shape[1]), jnp.float32) + offset_bias[None, :]
    for tap_index in range(tap_count):
        source = position - (tap_count - 1) + tap_index
        inside = (source >= first_token)[:, None]
        summed = summed + kernel[tap_index][None, :] * jnp.where(inside, padded[tap_index:tap_index + row_count].astype(jnp.float32), 0.0)
    return jax.nn.silu(summed).astype(jnp.bfloat16)

def end_state(x_stretch, b_stretch, step_stretch, cum_decay, request_of, inflow, entering, point):
    span = x_stretch.shape[0]
    head_count = x_stretch.shape[1]
    group_count = b_stretch.shape[1]
    within = jnp.arange(span)
    chosen = (request_of == request_of[point]) & (within <= point)
    point_weights = jnp.exp(jnp.where(chosen[:, None], cum_decay[point][None, :] - cum_decay, -jnp.inf)) * step_stretch
    scaled = (x_stretch.astype(jnp.float32) * point_weights[:, :, None]).astype(jnp.bfloat16)
    scaled = scaled.reshape(span, group_count, head_count // group_count, HEAD_DIM)
    summed = jnp.einsum('sghp,sgn->ghpn', scaled.astype(jnp.float32), b_stretch.astype(jnp.float32))
    return inflow[point][:, None, None] * entering + summed.reshape(head_count, HEAD_DIM, STATE)

def stretch_step(entering, pieces):
    x_stretch, b_stretch, c_stretch, step_stretch, log_decay, request_of, first_token, stretch_start = pieces
    span = x_stretch.shape[0]
    head_count = x_stretch.shape[1]
    group_count = b_stretch.shape[1]
    per_group = head_count // group_count
    cum_decay = jnp.cumsum(log_decay, axis=0)
    inflow = jnp.where((first_token < stretch_start)[:, None], jnp.exp(cum_decay), 0.0)
    within = jnp.arange(span)
    causal = (request_of[:, None] == request_of[None, :]) & (within[None, :] <= within[:, None])
    cum_heads = cum_decay.T
    decay = jnp.exp(jnp.where(causal[None], cum_heads[:, :, None] - cum_heads[:, None, :], -jnp.inf)) * step_stretch.T[:, None, :]
    c_wide = c_stretch.astype(jnp.float32)
    scores = jnp.einsum('tgn,sgn->gts', c_wide, b_stretch.astype(jnp.float32))
    weights = (scores[:, None] * decay.reshape(group_count, per_group, span, span)).astype(jnp.bfloat16)
    x_groups = x_stretch.reshape(span, group_count, per_group, HEAD_DIM)
    inner = jnp.einsum('ghts,sghp->tghp', weights.astype(jnp.float32), x_groups.astype(jnp.float32))
    carried = jnp.einsum('tgn,ghpn->tghp', c_wide, entering.reshape(group_count, per_group, HEAD_DIM, STATE), precision=lax.Precision.HIGHEST)
    inter = inflow.reshape(span, group_count, per_group)[..., None] * carried
    output = (inner + inter).reshape(span, head_count, HEAD_DIM)
    leaving = end_state(x_stretch, b_stretch, step_stretch, cum_decay, request_of, inflow, entering, span - 1)
    return (leaving, (output, entering))

def section(x_rows, bc_rows, z_rows, raw_step, conv_x_w, conv_x_b, conv_bc_w, conv_bc_b, a_log, dt_bias, skip_d, norm_gain, req_lengths):
    tok_count = x_rows.shape[0]
    group_width = bc_rows.shape[2]
    last_token = jnp.cumsum(req_lengths).astype(jnp.int32) - 1
    first_of_req = last_token - req_lengths + 1
    position = jnp.arange(tok_count, dtype=jnp.int32)
    request_of = lax.optimization_barrier(jnp.sum((last_token[None, :] < position[:, None]).astype(jnp.int32), axis=1))
    first_token = first_of_req[request_of]
    bc_flat = bc_rows.reshape(tok_count, 2 * group_width)
    pad_x = jnp.concatenate([jnp.zeros((KW - 1, x_rows.shape[1]), x_rows.dtype), x_rows], axis=0)
    pad_bc = jnp.concatenate([jnp.zeros((KW - 1, 2 * group_width), bc_flat.dtype), bc_flat], axis=0)
    x_conv = conv_silu(pad_x, conv_x_w, conv_x_b, position, first_token)
    bc_conv = conv_silu(pad_bc, conv_bc_w.reshape(KW, 2 * group_width), conv_bc_b.reshape(2 * group_width), position, first_token)
    step_size = jax.nn.softplus(raw_step + dt_bias[None, :])
    log_decay = -jnp.exp(a_log)[None, :] * step_size
    stretch_count = tok_count // STRETCH
    x_stretches = x_conv.reshape(stretch_count, STRETCH, SCAN_LANE_COUNT, HEAD_DIM)
    b_stretches = bc_conv[:, :group_width].reshape(stretch_count, STRETCH, GROUPS, STATE)
    c_stretches = bc_conv[:, group_width:].reshape(stretch_count, STRETCH, GROUPS, STATE)
    step_stretches = step_size.reshape(stretch_count, STRETCH, SCAN_LANE_COUNT)
    decay_stretches = log_decay.reshape(stretch_count, STRETCH, SCAN_LANE_COUNT)
    req_stretches = request_of.reshape(stretch_count, STRETCH)
    first_stretches = first_token.reshape(stretch_count, STRETCH)
    stretch_starts = STRETCH * jnp.arange(stretch_count, dtype=jnp.int32)
    start_state = jnp.zeros((SCAN_LANE_COUNT, HEAD_DIM, STATE), jnp.float32)
    leaving, (outputs, entered) = lax.scan(stretch_step, start_state, (x_stretches, b_stretches, c_stretches, step_stretches, decay_stretches, req_stretches, first_stretches, stretch_starts))
    mixed_f = outputs.reshape(tok_count, SCAN_LANE_COUNT, HEAD_DIM) + skip_d[None, :, None] * x_conv.reshape(tok_count, SCAN_LANE_COUNT, HEAD_DIM).astype(jnp.float32)
    gated = mixed_f.reshape(tok_count, DIN) * jax.nn.silu(z_rows.astype(jnp.float32))
    grouped = gated.reshape(tok_count, GROUPS, DIN // GROUPS)
    norm_scale = lax.rsqrt(lax.optimization_barrier(jnp.mean(grouped * grouped, axis=2, keepdims=True)) + EPS)
    mixed = ((grouped * norm_scale).reshape(tok_count, DIN) * norm_gain[None, :]).astype(jnp.bfloat16)

    def request_state(request):
        point = last_token[request]
        stretch_index = point // STRETCH
        inside_point = point - stretch_index * STRETCH
        cum_decay = jnp.cumsum(decay_stretches[stretch_index], axis=0)
        inflow = jnp.where((first_stretches[stretch_index] < stretch_index * STRETCH)[:, None], jnp.exp(cum_decay), 0.0)
        return end_state(x_stretches[stretch_index], b_stretches[stretch_index], step_stretches[stretch_index], cum_decay, req_stretches[stretch_index], inflow, entered[stretch_index], inside_point)
    finals = lax.map(request_state, jnp.arange(REQS, dtype=jnp.int32))

    def request_tail(request):
        point = last_token[request]
        rows_x = lax.dynamic_slice_in_dim(pad_x, (point + 1).astype(jnp.int32), KW - 1, 0)
        rows_bc = lax.dynamic_slice_in_dim(pad_bc, (point + 1).astype(jnp.int32), KW - 1, 0)
        source = point - (KW - 2) + jnp.arange(KW - 1, dtype=jnp.int32)
        inside = (source >= first_of_req[request])[:, None]
        zero_value = jnp.zeros((), jnp.bfloat16)
        return (jnp.where(inside, rows_x, zero_value), jnp.where(inside, rows_bc, zero_value))
    tail_x, tail_bc = lax.map(request_tail, jnp.arange(REQS, dtype=jnp.int32))
    tail_bc = tail_bc.reshape(REQS, KW - 1, 2, group_width)
    return (mixed, finals, tail_x, tail_bc)

def reference(x_in, bc_in, z_in, dt_in, conv_x_w, conv_x_b, conv_bc_w, conv_bc_b, a_log, dt_bias, skip_d, norm_gain, lengths, owner_slot):
    results = []
    for side_index in range(2):
        results.append(section(x_in[side_index], bc_in[side_index], z_in[side_index], dt_in[side_index], conv_x_w, conv_x_b, conv_bc_w, conv_bc_b, a_log, dt_bias, skip_d, norm_gain, lengths[side_index]))
    placed = []
    for side_index in range(2):
        opposite = 1 - side_index
        slot_order = owner_slot[opposite]
        placed.append(tuple((jnp.zeros_like(member).at[slot_order].set(member) for member in results[opposite][1:])))
    mixed = jnp.stack([results[0][0], results[1][0]])
    handed_state = jnp.stack([placed[0][0], placed[1][0]])
    handed_tail_x = jnp.stack([placed[0][1], placed[1][1]])
    handed_tail_bc = jnp.stack([placed[0][2], placed[1][2]])
    return (mixed, handed_state, handed_tail_x, handed_tail_bc)
```

```python
import functools

import jax
import jax.numpy as jnp
from jax import lax
from jax.experimental import pallas as pl
from jax.experimental.pallas import tpu as pltpu
from jax.sharding import PartitionSpec as P

HEAD_DIM = 64
STATE = 128
STRETCH = 128
LANES = 128
HALO = 16
KW = 4
EPS = 1e-05
BF = jnp.bfloat16
F32 = jnp.float32
I32 = jnp.int32
VMEM_LIMIT = 48 * 1024 * 1024

TOK = 512
NC = TOK // STRETCH
WIDTH = 2048
HEADS = WIDTH // HEAD_DIM
GROUPS = 2
GWIDTH = WIDTH // GROUPS
BCW = 512
REQS = 32
STEPS = 4
SW = WIDTH // STEPS
SLT = SW // LANES
ROWS_A = NC * STRETCH + 2 * STRETCH + 16
PIECE = 3 * 64 + 16
BACK = 64 + 16


def shift_in(block, distance):
    count = lax.axis_size("ctx")
    return lax.ppermute(block, "ctx", [(i, i + distance) for i in range(count - distance)])


def swish(v):
    half = 0.5 * v
    return half + half * jnp.tanh(half)


def split3(v, lane):
    hi = v.astype(BF).astype(F32)
    rest = v - hi
    mid = rest.astype(BF).astype(F32)
    low = rest - mid
    return jnp.where(
        lane < HEADS, hi, jnp.where(lane < 2 * HEADS, mid, jnp.where(lane < 3 * HEADS, low, 0.0))
    ).astype(BF)


def spread_matrix(first_head, width):
    row = lax.broadcasted_iota(I32, (LANES, width), 0)
    col = lax.broadcasted_iota(I32, (LANES, width), 1)
    same = ((row & (HEADS - 1)) == (col >> 6) + first_head) & (row < 3 * HEADS)
    return jnp.where(same, 1.0, 0.0).astype(BF)


def conv_tile(ext, taps, bias, masks):
    acc = bias + taps[KW - 1] * ext[HALO:]
    for d in range(1, KW):
        acc = acc + taps[KW - 1 - d] * (pltpu.roll(ext, d, 0)[HALO:] * masks[d - 1])
    return swish(acc)


def stage_a(
    idx_ref, len_ref, x_ref, xh_ref, bc_ref, bch_ref, dt_ref, wx_ref, bx_ref, wbc_ref, bbc_ref,
    al_ref, db_ref,
    piece_ref, s_ref, d_ref, eg_ref, ent_ref, xc_ref, bcc_ref, cum_ref, step_ref, fl_ref,
    mask_scr, wst_scr, spread_scr, bt_scr, entf_scr, first_scr, sc_scr,
):
    s = pl.program_id(0)
    lane = lax.broadcasted_iota(I32, (STRETCH, LANES), 1)
    row = lax.broadcasted_iota(I32, (STRETCH, LANES), 0)

    @pl.when(s == 0)
    def _():
        start = -idx_ref[0] * TOK
        zero = jnp.int32(0)

        def scan(r, carry):
            first, count, e0, f0, e1, f1, fa = carry
            last = first + len_ref[0, r] - 1
            first_scr[r] = first
            ends = (last >= 0) & (last < TOK)
            take0, take1 = ends & (count == 0), ends & (count == 1)
            fa = tuple(
                jnp.where(
                    (first <= c * STRETCH + STRETCH - 1) & (last >= c * STRETCH + STRETCH - 1),
                    first,
                    fa[c],
                )
                for c in range(NC)
            )
            return (
                last + 1,
                count + jnp.where(ends, 1, 0),
                jnp.where(take0, last, e0),
                jnp.where(take0, first, f0),
                jnp.where(take1, last, e1),
                jnp.where(take1, first, f1),
                fa,
            )

        _, _, e0, f0, e1, f1, fa = lax.fori_loop(
            0, REQS, scan, (start, zero, zero, zero, zero, zero, (zero,) * NC)
        )
        sc_scr[0], sc_scr[1], sc_scr[2], sc_scr[3] = e0, f0, e1, f1

        for c in range(NC):
            rows = pl.ds(c * STRETCH, STRETCH)
            here = row + c * STRETCH

            def later(r, fl):
                return jnp.where(here >= first_scr[r], first_scr[r], fl)

            fl = lax.fori_loop(0, REQS, later, jnp.full((STRETCH, LANES), start, I32))
            fl_ref[rows, :] = fl
            for d in range(1, KW):
                mask_scr[d - 1, rows, :] = jnp.where(here - fl >= d, 1.0, 0.0)

        raw = dt_ref[...] + db_ref[...]
        step = jnp.maximum(raw, 0.0) + jnp.log1p(jnp.exp(-jnp.abs(raw)))
        step_ref[...] = step
        log_decay = -jnp.exp(al_ref[...]) * step
        lower = jnp.where(row >= lane, 1.0, 0.0)
        for c in range(NC):
            cum_ref[c * STRETCH : (c + 1) * STRETCH, :] = jnp.dot(
                lower,
                log_decay[c * STRETCH : (c + 1) * STRETCH, :],
                precision=lax.Precision.HIGHEST,
                preferred_element_type=F32,
            )
        through = []
        for c in range(NC):
            rows = slice(c * STRETCH, (c + 1) * STRETCH)
            cum = cum_ref[rows, :]
            end = cum[STRETCH - 1 :, :]
            w = jnp.where(row + c * STRETCH >= fa[c], jnp.exp(end - cum) * step_ref[rows, :], 0.0)
            wst_scr[rows, :] = split3(w, lane)
            through.append(jnp.where(fa[c] < c * STRETCH, jnp.exp(end), 0.0))
        inflow_end = []
        for k, (e, f) in enumerate(((e0, f0), (e1, f1))):
            base = pl.multiple_of((e >> 7) * STRETCH, STRETCH)
            here = row + base
            end = cum_ref[pl.ds(e, 1), :]
            w = jnp.exp(end - cum_ref[pl.ds(base, STRETCH), :]) * step_ref[pl.ds(base, STRETCH), :]
            w = jnp.where((here >= f) & (here <= e), w, 0.0)
            at = (NC + k) * STRETCH
            wst_scr[at : at + STRETCH, :] = split3(w, lane)
            inflow_end.append(jnp.where(f < base, jnp.exp(end), 0.0))
        gains = [jnp.ones((1, LANES), F32)]
        for c in range(NC):
            gains.append(gains[-1] * through[c])
        gain_end = gains[0]
        for c in range(1, NC):
            gain_end = jnp.where((e0 >> 7) == c, gains[c], gain_end)
        extra = jnp.zeros((16, LANES), F32)
        row16 = lax.broadcasted_iota(I32, (16, LANES), 0)
        lane16 = lax.broadcasted_iota(I32, (16, LANES), 1)
        for i, v in enumerate(through + gains[:NC] + inflow_end + [gain_end * inflow_end[0], gains[NC]]):
            extra = jnp.where(row16 == i, v, extra)
        wst_scr[(NC + 2) * STRETCH :, :] = split3(extra, lane16)

        for part in range(2):
            for g in range(GROUPS):
                at = slice((part * GROUPS + g) * LANES, (part * GROUPS + g + 1) * LANES)
                own = slice(g * LANES, (g + 1) * LANES)
                taps = [wbc_ref[k, part : part + 1, own] for k in range(KW)]
                bias = bbc_ref[part : part + 1, own]
                for c in range(NC):
                    if c == 0:
                        ext = jnp.concatenate([bch_ref[:, at], bc_ref[0:STRETCH, at]], axis=0)
                    else:
                        ext = bc_ref[c * STRETCH - HALO : (c + 1) * STRETCH, at]
                    rows = slice(c * STRETCH, (c + 1) * STRETCH)
                    masks = [mask_scr[d, rows, :] for d in range(KW - 1)]
                    out = conv_tile(ext.astype(F32), taps, bias, masks).astype(BF)
                    bcc_ref[rows, at] = out
                    if part == 0:
                        bt_scr[g * NC + c] = out.astype(F32).T.astype(BF)

    e0, f0, e1, f1 = sc_scr[0], sc_scr[1], sc_scr[2], sc_scr[3]
    spread_scr[...] = jnp.dot(
        wst_scr[...], spread_matrix(s * (SW // HEAD_DIM), SW), preferred_element_type=F32
    )
    ex = (NC + 2) * STRETCH
    group = s // (STEPS // GROUPS)
    d_ref[...] = jnp.broadcast_to(spread_scr[ex + 11 : ex + 12, :], (8, SW))
    eg_ref[...] = spread_scr[ex : ex + 8, :]
    for c in range(NC):
        rows = slice(c * STRETCH, (c + 1) * STRETCH)
        masks = [mask_scr[d, rows, :] for d in range(KW - 1)]
        scaled = []
        for t in range(SLT):
            at = slice(t * LANES, (t + 1) * LANES)
            if c == 0:
                ext = jnp.concatenate([xh_ref[:, at], x_ref[0:STRETCH, at]], axis=0)
            else:
                ext = x_ref[c * STRETCH - HALO : (c + 1) * STRETCH, at]
            taps = [wx_ref[k : k + 1, at] for k in range(KW)]
            out = conv_tile(ext.astype(F32), taps, bx_ref[:, at], masks).astype(BF)
            xc_ref[rows, at] = out
            scaled.append((out.astype(F32) * spread_scr[rows, at]).astype(BF))
        local = jnp.dot(
            bt_scr[group * NC + c], jnp.concatenate(scaled, axis=1), preferred_element_type=F32
        )
        if c == 0:
            entf_scr[0] = jnp.zeros((STATE, SW), F32)
            ent_ref[0] = jnp.zeros((STATE, SW), BF)
            entering = local
        else:
            entering = spread_scr[ex + c : ex + c + 1, :] * entf_scr[c] + local
        if c < NC - 1:
            entf_scr[c + 1] = entering
            ent_ref[c + 1] = entering.astype(BF)
        else:
            leaving = entering.astype(BF)
            s_ref[...] = leaving
            for j in range(2 * SLT):
                piece_ref[j, 128:192, :] = leaving[
                    (j % 2) * 64 : (j % 2) * 64 + 64, (j // 2) * LANES : (j // 2 + 1) * LANES
                ]
    for k, e in enumerate((e0, e1)):
        c = e >> 7
        base = pl.multiple_of(c * STRETCH, STRETCH)
        at = (NC + k) * STRETCH
        scaled = (
            xc_ref[pl.ds(base, STRETCH), :].astype(F32) * spread_scr[at : at + STRETCH, :]
        ).astype(BF)
        final = spread_scr[ex + 8 + k : ex + 9 + k, :] * entf_scr[c] + jnp.dot(
            bt_scr[group * NC + c], scaled, preferred_element_type=F32
        )
        final = final.astype(BF)
        for j in range(2 * SLT):
            piece_ref[j, k * 64 : k * 64 + 64, :] = final[
                (j % 2) * 64 : (j % 2) * 64 + 64, (j // 2) * LANES : (j // 2 + 1) * LANES
            ]

    tails_x, tails_bc = [], []
    pick_row = lax.broadcasted_iota(I32, (16, 2 * HALO), 0)
    pick_col = lax.broadcasted_iota(I32, (16, 2 * HALO), 1)
    for e, f in ((e0, f0), (e1, f1)):
        base = pl.multiple_of((e >> 4) * HALO, HALO)
        before = pl.multiple_of(jnp.maximum(base - HALO, 0), HALO)
        source = e - (KW - 2) + pick_row
        pick = (pick_col + base - HALO == source) & (source >= f) & (pick_row < KW - 1)
        pick = jnp.where(pick, 1.0, 0.0).astype(BF)

        def tail(ref, halo_ref):
            head = jnp.where(base > 0, ref[pl.ds(before, HALO), :], halo_ref[...])
            window = jnp.concatenate([head, ref[pl.ds(base, HALO), :]], axis=0)
            return jnp.dot(pick, window, preferred_element_type=F32)

        tails_x.append(tail(x_ref, xh_ref))
        tails_bc.append(tail(bc_ref, bch_ref))
    row16 = lax.broadcasted_iota(I32, (16, LANES), 0)
    for t in range(SLT):
        at = slice(t * LANES, (t + 1) * LANES)
        gain_hi = spread_scr[ex + 10 : ex + 11, at].astype(BF).astype(F32)
        gain_lo = spread_scr[ex + 10 : ex + 11, at] - gain_hi
        pass_hi = spread_scr[ex + 11 : ex + 12, at].astype(BF).astype(F32)
        pass_lo = spread_scr[ex + 11 : ex + 12, at] - pass_hi
        bc_rows = []
        for k in range(2):
            one = tails_bc[k][:, at]
            bc_rows.append(jnp.sum(jnp.where(row16 == s, one, 0.0), axis=0, keepdims=True))
        for half in range(2):
            block = jnp.zeros((16, LANES), F32)
            values = [gain_hi, gain_lo, pass_hi, pass_lo]
            for k in range(2):
                one = tails_x[k][:, at]
                values += [one[0:1], one[1:2]] if half == 0 else [one[2:3], bc_rows[k]]
            for i, v in enumerate(values):
                block = jnp.where(row16 == i, v, block)
            piece_ref[2 * t + half, 192:208, :] = block.astype(BF)


def stage_b(xc_ref, bcc_ref, cum_ref, step_ref, fl_ref, skip_ref, y_ref):
    c = pl.program_id(0)
    row = lax.broadcasted_iota(I32, (STRETCH, LANES), 0)
    lane = lax.broadcasted_iota(I32, (STRETCH, LANES), 1)
    keep = (lane <= row) & (lane + c * STRETCH >= fl_ref[...])
    cum = cum_ref[...]
    cum_t = cum.T
    step_t = step_ref[...].T
    low = lax.broadcasted_iota(I32, (STRETCH, LANES), 1) < HEAD_DIM
    for g in range(GROUPS):
        b = bcc_ref[:, g * LANES : (g + 1) * LANES]
        cc = bcc_ref[:, (GROUPS + g) * LANES : (GROUPS + g + 1) * LANES]
        scores = lax.dot_general(cc, b, (((1,), (1,)), ((), ())), preferred_element_type=F32)
        for i in range(HEADS // GROUPS // 2):
            pair = g * (HEADS // GROUPS // 2) + i
            weights = []
            for h in (2 * pair, 2 * pair + 1):
                decay = jnp.exp(jnp.where(keep, cum[:, h : h + 1] - cum_t[h : h + 1, :], -jnp.inf))
                weights.append((scores * (decay * step_t[h : h + 1, :])).astype(BF))
            at = slice(pair * LANES, (pair + 1) * LANES)
            x = xc_ref[:, at]
            xf = x.astype(F32)
            both = jnp.concatenate(
                [jnp.where(low, xf, 0.0).astype(BF), jnp.where(low, 0.0, xf).astype(BF)], axis=0
            )
            inner = jnp.dot(
                jnp.concatenate(weights, axis=1), both, preferred_element_type=F32
            )
            y_ref[:, at] = inner + skip_ref[:, at] * xf


def stage_c(
    y_ref, z_ref, c_ref, ent_ref, s1_ref, s2_ref, d1_ref, eg_ref, cum_ref, fl_ref, gain_ref, out_ref
):
    g, c = pl.program_id(0), pl.program_id(1)
    lane = lax.broadcasted_iota(I32, (STRETCH, LANES), 1)
    inflow = jnp.where(fl_ref[...] < c * STRETCH, jnp.exp(cum_ref[...]), 0.0)
    wide = jnp.dot(
        split3(inflow, lane),
        spread_matrix(g * (HEADS // GROUPS), GWIDTH),
        preferred_element_type=F32,
    )
    incoming = s1_ref[...].astype(F32) + d1_ref[0:1, :] * s2_ref[...].astype(F32)
    entering = ent_ref[0].astype(F32) + eg_ref[pl.ds(NC + c, 1), :] * incoming
    carried = jnp.dot(c_ref[...], entering.astype(BF), preferred_element_type=F32)
    gated = (y_ref[...] + wide * carried) * swish(z_ref[...].astype(F32))
    mean = jnp.sum(gated * gated, axis=1, keepdims=True) * (1.0 / GWIDTH)
    out_ref[...] = (gated * lax.rsqrt(mean + EPS) * gain_ref[...]).astype(BF)


def combine(len_ref, owner_ref, got_ref, out_ref):
    row16 = lax.broadcasted_iota(I32, (16, LANES), 0)

    def one(r, carry):
        first, before = carry
        last = first + len_ref[0, r] - 1
        home = last >> 9
        second = before == home
        h1, h2 = jnp.maximum(home - 1, 0), jnp.maximum(home - 2, 0)
        slot = owner_ref[0, r]
        extra = got_ref[home, 192:208, :].astype(F32)
        extra1 = got_ref[h1, 192:208, :].astype(F32)
        gain = jnp.where(second, 0.0, extra[0:1] + extra[1:2])
        passing = extra1[2:3] + extra1[3:4]
        k = pl.multiple_of(jnp.where(second, 64, 0), 64)
        own = got_ref[home, pl.ds(k, 64), :].astype(F32)
        s1 = got_ref[h1, 128:192, :].astype(F32)
        s2 = got_ref[h2, 128:192, :].astype(F32)
        out_ref[slot, 0:64, :] = (own + gain * (s1 + passing * s2)).astype(BF)
        tail = jnp.where(second, pltpu.roll(extra, 10, 0), pltpu.roll(extra, 12, 0))
        out_ref[slot, 64:80, :] = jnp.where(row16 < 2, tail, 0.0).astype(BF)
        return last + 1, home

    lax.fori_loop(0, REQS, one, (jnp.int32(0), jnp.int32(-1)), unroll=2)


def finish(got_ref, state_ref, tx_ref, tbc_ref):
    tails = [got_ref[j, 64:80, :].astype(F32) for j in range(REQS)]
    for t in range(WIDTH // LANES):
        at = slice(t * LANES, (t + 1) * LANES)
        block = jnp.concatenate(
            [got_ref[2 * t, 0:64, :], got_ref[2 * t + 1, 0:64, :]], axis=0
        ).astype(F32)
        turned = block.T
        state_ref[2 * t] = turned[0:64]
        state_ref[2 * t + 1] = turned[64:128]
        tx_ref[:, at] = jnp.concatenate([tails[2 * t][0:2], tails[2 * t + 1][0:1]], axis=0).astype(BF)
    for k in range(KW - 1):
        for q in range(4):
            value = tails[2 * (4 * k + q) + 1][1:2].astype(BF)
            tbc_ref[k, q // 2 : q // 2 + 1, (q % 2) * LANES : (q % 2 + 1) * LANES] = value


def call(kernel, grid, ins, outs, scratch=(), flops=0, nbytes=0):
    return pl.pallas_call(
        kernel,
        grid=grid,
        in_specs=ins,
        out_specs=[o[1] for o in outs],
        out_shape=[o[0] for o in outs],
        scratch_shapes=list(scratch),
        compiler_params=pltpu.CompilerParams(vmem_limit_bytes=VMEM_LIMIT),
        cost_estimate=pl.CostEstimate(flops=flops, bytes_accessed=nbytes, transcendentals=0),
    )


def whole(*shape):
    return pl.BlockSpec(shape, lambda *_: (0,) * len(shape))


def on_device(
    x_in, bc_in, z_in, dt_in, conv_x_w, conv_x_b, conv_bc_w, conv_bc_b, a_log, dt_bias, skip_d,
    norm_gain, lengths, owner_slot,
):
    x = x_in[0]
    bc = bc_in[0].reshape(TOK, BCW)
    z = z_in[0]
    halo = shift_in(jnp.concatenate([x[TOK - HALO :], bc[TOK - HALO :]], axis=1), 1)
    dt = jnp.tile(dt_in[0], (1, 4))
    a_row = jnp.tile(a_log, 4).reshape(1, LANES)
    bias_row = jnp.tile(dt_bias, 4).reshape(1, LANES)
    index = lax.axis_index("ctx").astype(I32).reshape(1)
    smem = pl.BlockSpec(memory_space=pltpu.SMEM)
    shape = jax.ShapeDtypeStruct

    pieces, left, passing, entry, ent, xc, bcc, cum, step, fl = call(
        stage_a,
        (STEPS,),
        [
            smem,
            smem,
            pl.BlockSpec((TOK, SW), lambda s: (0, s)),
            pl.BlockSpec((HALO, SW), lambda s: (0, s)),
            whole(TOK, BCW),
            pl.BlockSpec((HALO, BCW), lambda s: (0, WIDTH // BCW)),
            whole(TOK, LANES),
            pl.BlockSpec((KW, SW), lambda s: (0, s)),
            pl.BlockSpec((1, SW), lambda s: (0, s)),
            whole(KW, 2, 2 * LANES),
            whole(2, 2 * LANES),
            whole(1, LANES),
            whole(1, LANES),
        ],
        [
            (shape((32, PIECE, LANES), BF), pl.BlockSpec((2 * SLT, PIECE, LANES), lambda s: (s, 0, 0))),
            (shape((STATE, WIDTH), BF), pl.BlockSpec((STATE, SW), lambda s: (0, s))),
            (shape((8, WIDTH), F32), pl.BlockSpec((8, SW), lambda s: (0, s))),
            (shape((8, WIDTH), F32), pl.BlockSpec((8, SW), lambda s: (0, s))),
            (shape((NC, STATE, WIDTH), BF), pl.BlockSpec((NC, STATE, SW), lambda s: (0, 0, s))),
            (shape((TOK, WIDTH), BF), pl.BlockSpec((TOK, SW), lambda s: (0, s))),
            (shape((TOK, BCW), BF), whole(TOK, BCW)),
            (shape((TOK, LANES), F32), whole(TOK, LANES)),
            (shape((TOK, LANES), F32), whole(TOK, LANES)),
            (shape((TOK, LANES), I32), whole(TOK, LANES)),
        ],
        [
            pltpu.VMEM((KW - 1, TOK, LANES), F32),
            pltpu.VMEM((ROWS_A, LANES), BF),
            pltpu.VMEM((ROWS_A, SW), F32),
            pltpu.VMEM((GROUPS * NC, STATE, STRETCH), BF),
            pltpu.VMEM((NC, STATE, SW), F32),
            pltpu.SMEM((REQS,), I32),
            pltpu.SMEM((4,), I32),
        ],
        flops=2 * 10**9,
        nbytes=10 * 2**20,
    )(
        index, lengths, x, halo, bc, halo, dt, conv_x_w, conv_x_b.reshape(1, WIDTH), conv_bc_w,
        conv_bc_b, a_row, bias_row,
    )

    got = lax.all_to_all(pieces, "ctx", split_axis=0, concat_axis=0, tiled=True)
    s1 = shift_in(left, 1)
    s2 = shift_in(left, 2)
    d1 = shift_in(passing, 1)

    (y,) = call(
        stage_b,
        (NC,),
        [
            pl.BlockSpec((STRETCH, WIDTH), lambda c: (c, 0)),
            pl.BlockSpec((STRETCH, BCW), lambda c: (c, 0)),
            pl.BlockSpec((STRETCH, LANES), lambda c: (c, 0)),
            pl.BlockSpec((STRETCH, LANES), lambda c: (c, 0)),
            pl.BlockSpec((STRETCH, LANES), lambda c: (c, 0)),
            whole(1, WIDTH),
        ],
        [(shape((TOK, WIDTH), F32), pl.BlockSpec((STRETCH, WIDTH), lambda c: (c, 0)))],
        flops=10**9,
        nbytes=20 * 2**20,
    )(xc, bcc, cum, step, fl, jnp.repeat(skip_d, HEAD_DIM).reshape(1, WIDTH))

    (back,) = call(
        combine,
        (),
        [smem, smem, pl.BlockSpec(memory_space=pltpu.VMEM)],
        [(shape((REQS, BACK, LANES), BF), pl.BlockSpec(memory_space=pltpu.VMEM))],
        flops=10**7,
        nbytes=3 * 2**20,
    )(lengths, owner_slot, got)
    own = lax.all_to_all(back, "ctx", split_axis=0, concat_axis=0, tiled=True)

    by_c = lambda g, c: (c, 0)
    by_g = lambda g, c: (0, g)
    by_cg = lambda g, c: (c, g)
    (mixed,) = call(
        stage_c,
        (GROUPS, NC),
        [
            pl.BlockSpec((STRETCH, GWIDTH), by_cg),
            pl.BlockSpec((STRETCH, GWIDTH), by_cg),
            pl.BlockSpec((STRETCH, LANES), lambda g, c: (c, GROUPS + g)),
            pl.BlockSpec((1, STATE, GWIDTH), lambda g, c: (c, 0, g)),
            pl.BlockSpec((STATE, GWIDTH), by_g),
            pl.BlockSpec((STATE, GWIDTH), by_g),
            pl.BlockSpec((8, GWIDTH), by_g),
            pl.BlockSpec((8, GWIDTH), by_g),
            pl.BlockSpec((STRETCH, LANES), by_c),
            pl.BlockSpec((STRETCH, LANES), by_c),
            pl.BlockSpec((1, GWIDTH), by_g),
        ],
        [(shape((TOK, WIDTH), BF), pl.BlockSpec((STRETCH, GWIDTH), by_cg))],
        flops=10**9,
        nbytes=15 * 2**20,
    )(y, z, bcc, ent, s1, s2, d1, entry, cum, fl, norm_gain.reshape(1, WIDTH))

    swapped = lax.ppermute(own, "side", [(0, 1), (1, 0)])
    state, tail_x, tail_bc = call(
        finish,
        (),
        [pl.BlockSpec(memory_space=pltpu.VMEM)],
        [
            (shape((HEADS, HEAD_DIM, STATE), F32), pl.BlockSpec(memory_space=pltpu.VMEM)),
            (shape((KW - 1, WIDTH), BF), pl.BlockSpec(memory_space=pltpu.VMEM)),
            (shape((KW - 1, 2, 2 * LANES), BF), pl.BlockSpec(memory_space=pltpu.VMEM)),
        ],
        flops=10**7,
        nbytes=3 * 2**20,
    )(swapped)
    return mixed[None], state[None, None], tail_x[None, None], tail_bc[None, None]


def solution(mesh):
    placed = (
        P("side", "ctx", "head"),
        P("side", "ctx", None, "head"),
        P("side", "ctx", "head"),
        P("side", "ctx", "head"),
        P(None, "head"),
        P("head"),
        P(None, None, "head"),
        P(None, "head"),
        P("head"),
        P("head"),
        P("head"),
        P("head"),
        P("side", None),
        P("side", None),
    )
    return jax.shard_map(
        on_device,
        mesh=mesh,
        in_specs=placed,
        out_specs=(
            P("side", "ctx", "head"),
            P("side", "ctx", "head", None, None),
            P("side", "ctx", None, "head"),
            P("side", "ctx", None, None, "head"),
        ),
        check_vma=False,
    )
```

```python
import jax
import jax.numpy as jnp
from jax import lax
from jax.experimental import pallas as pl
from jax.experimental.pallas import tpu as pltpu
from jax.sharding import PartitionSpec as P

HEAD_DIM = 64
STATE = 128
STRETCH = 128
LANES = 128
HALO = 16
KW = 4
EPS = 1e-05
BF = jnp.bfloat16
F32 = jnp.float32
I32 = jnp.int32
LARGE = 60 * 1024 * 1024
SMALL = 16 * 1024 * 1024

TOK = 512
NC = TOK // STRETCH
WIDTH = 2048
HEADS = WIDTH // HEAD_DIM
GROUPS = 2
GWIDTH = WIDTH // GROUPS
BCW = 512
REQS = 32
STEPS = 4
SW = WIDTH // STEPS
SLT = SW // LANES
PIECE = 2 * 64 + 16
BACK = 64 + 16


def shift_in(block, distance):
    count = lax.axis_size("ctx")
    return lax.ppermute(block, "ctx", [(i, i + distance) for i in range(count - distance)])


def swish(v):
    half = 0.5 * v
    return half + half * jnp.tanh(half)


def split3(v, lane):
    hi = v.astype(BF).astype(F32)
    rest = v - hi
    mid = rest.astype(BF).astype(F32)
    low = rest - mid
    return jnp.where(
        lane < HEADS, hi, jnp.where(lane < 2 * HEADS, mid, jnp.where(lane < 3 * HEADS, low, 0.0))
    ).astype(BF)


def spread_matrix(first_head, width):
    row = lax.broadcasted_iota(I32, (LANES, width), 0)
    col = lax.broadcasted_iota(I32, (LANES, width), 1)
    same = ((row & (HEADS - 1)) == (col >> 6) + first_head) & (row < 3 * HEADS)
    return jnp.where(same, 1.0, 0.0).astype(BF)


def conv_tile(ext, taps, bias, masks):
    acc = bias + taps[KW - 1] * ext[HALO:]
    for d in range(1, KW):
        acc = acc + taps[KW - 1 - d] * (pltpu.roll(ext, d, 0)[HALO:] * masks[d - 1])
    return swish(acc)


def scan_lengths(idx_ref, len_ref, first_scr=None):
    zero = jnp.int32(0)

    def scan(r, carry):
        first, count, behind, e0, f0, e1, f1, fa = carry
        last = first + len_ref[0, r] - 1
        if first_scr is not None:
            first_scr[r] = first
        ends = (last >= 0) & (last < TOK)
        take0, take1 = ends & (count == 0), ends & (count == 1)
        points = [c * STRETCH + STRETCH - 1 for c in range(NC)]
        fa = tuple(
            jnp.where((first <= p) & (last >= p), first, old) for p, old in zip(points, fa)
        )
        return (
            last + 1,
            count + jnp.where(ends, 1, 0),
            behind + jnp.where((last >= -TOK) & (last < 0), 1, 0),
            jnp.where(take0, last, e0),
            jnp.where(take0, first, f0),
            jnp.where(take1, last, e1),
            jnp.where(take1, first, f1),
            fa,
        )

    start = -idx_ref[0] * TOK
    out = lax.fori_loop(
        0, REQS, scan, (start, zero, zero, zero, zero, zero, zero, (zero,) * NC), unroll=4
    )
    return out[1:]


def stretch_gains(cum_ref, fa):
    through = []
    gains = [jnp.ones((1, LANES), F32)]
    for c in range(NC):
        end = cum_ref[(c + 1) * STRETCH - 1 : (c + 1) * STRETCH, :]
        through.append(jnp.where(fa[c] < c * STRETCH, jnp.exp(end), 0.0))
        gains.append(gains[-1] * through[-1])
    return through, gains


def as_rows(values):
    row16 = lax.broadcasted_iota(I32, (16, LANES), 0)
    block = jnp.zeros((16, LANES), F32)
    for i, v in enumerate(values):
        block = jnp.where(row16 == i, v, block)
    return block


def stage_p(
    idx_ref, len_ref, dt_ref, al_ref, db_ref, cum_ref, step_ref, fl_ref, wst_ref, first_scr
):
    lane = lax.broadcasted_iota(I32, (STRETCH, LANES), 1)
    row = lax.broadcasted_iota(I32, (STRETCH, LANES), 0)
    fa = scan_lengths(idx_ref, len_ref, first_scr)[-1]
    start = -idx_ref[0] * TOK
    coef = -jnp.exp(jnp.concatenate([al_ref[...]] * 4, axis=1))
    bias = jnp.concatenate([db_ref[...]] * 4, axis=1)
    lower = jnp.where(row >= lane, 1.0, 0.0)
    for c in range(NC):
        rows = slice(c * STRETCH, (c + 1) * STRETCH)
        here = row + c * STRETCH

        def later(r, fl):
            return jnp.where(here >= first_scr[r], first_scr[r], fl)

        fl_ref[rows, :] = lax.fori_loop(
            0, REQS, later, jnp.full((STRETCH, LANES), start, I32), unroll=4
        )
        raw = jnp.concatenate([dt_ref[:, rows]] * 4, axis=0).T + bias
        step = jnp.maximum(raw, 0.0) + jnp.log1p(jnp.exp(-jnp.abs(raw)))
        step_ref[rows, :] = step
        cum = jnp.dot(
            lower, coef * step, precision=lax.Precision.HIGHEST, preferred_element_type=F32
        )
        cum_ref[rows, :] = cum
        w = jnp.exp(cum[STRETCH - 1 :, :] - cum) * step
        wst_ref[rows, :] = split3(jnp.where(here >= fa[c], w, 0.0), lane)
    through, gains = stretch_gains(cum_ref, fa)
    lane16 = lax.broadcasted_iota(I32, (16, LANES), 1)
    wst_ref[NC * STRETCH :, :] = split3(as_rows(through + gains), lane16)


def stage_a(
    x_ref, xh_ref, bc_ref, bch_ref, wx_ref, bx_ref, wbc_ref, bbc_ref, fl_ref, wst_ref,
    xc_ref, bcc_ref, ent_ref, s_ref, entry_ref,
    mask_scr, spread_scr, bt_scr,
):
    s = pl.program_id(0)
    row = lax.broadcasted_iota(I32, (STRETCH, LANES), 0)

    @pl.when(s == 0)
    def _():
        for c in range(NC):
            rows = slice(c * STRETCH, (c + 1) * STRETCH)
            since = row + c * STRETCH - fl_ref[rows, :]
            for d in range(1, KW):
                mask_scr[d - 1, rows, :] = jnp.where(since >= d, 1.0, 0.0)
        for part in range(2):
            for g in range(GROUPS):
                at = slice((part * GROUPS + g) * LANES, (part * GROUPS + g + 1) * LANES)
                own = slice(g * LANES, (g + 1) * LANES)
                taps = [wbc_ref[k, part : part + 1, own] for k in range(KW)]
                off = bbc_ref[part : part + 1, own]
                for c in range(NC):
                    if c == 0:
                        ext = jnp.concatenate([bch_ref[:, at], bc_ref[0:STRETCH, at]], axis=0)
                    else:
                        ext = bc_ref[c * STRETCH - HALO : (c + 1) * STRETCH, at]
                    rows = slice(c * STRETCH, (c + 1) * STRETCH)
                    masks = [mask_scr[d, rows, :] for d in range(KW - 1)]
                    out = conv_tile(ext.astype(F32), taps, off, masks).astype(BF)
                    bcc_ref[rows, at] = out
                    if part == 0:
                        bt_scr[g * NC + c] = out.astype(F32).T.astype(BF)

    spread_scr[...] = jnp.dot(
        wst_ref[...], spread_matrix(s * (SW // HEAD_DIM), SW), preferred_element_type=F32
    )
    ex = NC * STRETCH
    group = s // (STEPS // GROUPS)
    entry_ref[...] = spread_scr[ex:, :]
    entering = None
    for c in range(NC):
        rows = slice(c * STRETCH, (c + 1) * STRETCH)
        masks = [mask_scr[d, rows, :] for d in range(KW - 1)]
        scaled = []
        for t in range(SLT):
            at = slice(t * LANES, (t + 1) * LANES)
            if c == 0:
                ext = jnp.concatenate([xh_ref[:, at], x_ref[0:STRETCH, at]], axis=0)
            else:
                ext = x_ref[c * STRETCH - HALO : (c + 1) * STRETCH, at]
            taps = [wx_ref[k : k + 1, at] for k in range(KW)]
            out = conv_tile(ext.astype(F32), taps, bx_ref[:, at], masks).astype(BF)
            xc_ref[rows, at] = out
            scaled.append((out.astype(F32) * spread_scr[rows, at]).astype(BF))
        local = jnp.dot(
            bt_scr[group * NC + c], jnp.concatenate(scaled, axis=1), preferred_element_type=F32
        )
        if c == 0:
            ent_ref[0] = jnp.zeros((STATE, SW), BF)
            entering = local
        else:
            ent_ref[c] = entering.astype(BF)
            entering = spread_scr[ex + c : ex + c + 1, :] * entering + local
    s_ref[...] = entering.astype(BF)


def stage_e(
    idx_ref, len_ref, x_ref, xh_ref, bc_ref, bch_ref, xc_ref, bcc_ref, cum_ref, step_ref, ent_ref,
    s_ref,
    piece_ref, gain_ref,
    wst_scr, spread_scr, sc_scr,
):
    s = pl.program_id(0)
    lane = lax.broadcasted_iota(I32, (STRETCH, LANES), 1)
    row = lax.broadcasted_iota(I32, (STRETCH, LANES), 0)
    ex = 2 * STRETCH

    @pl.when(s == 0)
    def _():
        count, behind, e0, f0, e1, f1, fa = scan_lengths(idx_ref, len_ref)
        sc_scr[0], sc_scr[1], sc_scr[2], sc_scr[3], sc_scr[4] = e0, f0, e1, f1, count
        inflow = []
        for k, (e, f) in enumerate(((e0, f0), (e1, f1))):
            base = pl.multiple_of((e >> 7) * STRETCH, STRETCH)
            here = row + base
            end = cum_ref[pl.ds(e, 1), :]
            w = jnp.exp(end - cum_ref[pl.ds(base, STRETCH), :]) * step_ref[pl.ds(base, STRETCH), :]
            w = jnp.where((here >= f) & (here <= e), w, 0.0)
            wst_scr[k * STRETCH : (k + 1) * STRETCH, :] = split3(w, lane)
            inflow.append(jnp.where(f < base, jnp.exp(end), 0.0))
        _, gains = stretch_gains(cum_ref, fa)
        gain = gains[0]
        for c in range(1, NC):
            gain = jnp.where((e0 >> 7) == c, gains[c], gain)
        gain = gain * inflow[0]
        by_owner = jnp.where((count > 0) & (behind == 0), gain, 0.0)
        by_sender = jnp.where(count == 0, gains[NC], jnp.where(behind == 0, 0.0, gain))
        lane16 = lax.broadcasted_iota(I32, (16, LANES), 1)
        wst_scr[ex:, :] = split3(as_rows(inflow + [by_owner, by_sender]), lane16)

    e0, f0, e1, f1 = sc_scr[0], sc_scr[1], sc_scr[2], sc_scr[3]
    spread_scr[...] = jnp.dot(
        wst_scr[...], spread_matrix(s * (SW // HEAD_DIM), SW), preferred_element_type=F32
    )
    gain_ref[...] = jnp.broadcast_to(spread_scr[ex + 3 : ex + 4, :], (8, SW))
    group = s // (STEPS // GROUPS)
    for k, e in enumerate((e0, e1)):
        c = e >> 7
        base = pl.multiple_of(c * STRETCH, STRETCH)
        at = k * STRETCH
        scaled = (
            xc_ref[pl.ds(base, STRETCH), :].astype(F32) * spread_scr[at : at + STRETCH, :]
        ).astype(BF)
        b = jnp.where(
            group == 0,
            bcc_ref[pl.ds(base, STRETCH), 0:LANES].astype(F32),
            bcc_ref[pl.ds(base, STRETCH), LANES : 2 * LANES].astype(F32),
        )
        final = spread_scr[ex + k : ex + k + 1, :] * ent_ref[c].astype(F32) + jnp.dot(
            b.T.astype(BF), scaled, preferred_element_type=F32
        )
        if k == 0:
            final = jnp.where(sc_scr[4] == 0, s_ref[...].astype(F32), final)
        final = final.astype(BF)
        for j in range(2 * SLT):
            piece_ref[j, k * 64 : k * 64 + 64, :] = final[
                (j % 2) * 64 : (j % 2) * 64 + 64, (j // 2) * LANES : (j // 2 + 1) * LANES
            ]

    tails_x, tails_bc = [], []
    pick_row = lax.broadcasted_iota(I32, (16, 2 * HALO), 0)
    pick_col = lax.broadcasted_iota(I32, (16, 2 * HALO), 1)
    for e, f in ((e0, f0), (e1, f1)):
        base = pl.multiple_of((e >> 4) * HALO, HALO)
        before = pl.multiple_of(jnp.maximum(base - HALO, 0), HALO)
        source = e - (KW - 2) + pick_row
        pick = (pick_col + base - HALO == source) & (source >= f) & (pick_row < KW - 1)
        pick = jnp.where(pick, 1.0, 0.0).astype(BF)

        def tail(ref, halo_ref):
            head = jnp.where(base > 0, ref[pl.ds(before, HALO), :], halo_ref[...])
            window = jnp.concatenate([head, ref[pl.ds(base, HALO), :]], axis=0)
            return jnp.dot(pick, window, preferred_element_type=F32)

        tails_x.append(tail(x_ref, xh_ref))
        tails_bc.append(tail(bc_ref, bch_ref))
    row16 = lax.broadcasted_iota(I32, (16, LANES), 0)
    for t in range(SLT):
        at = slice(t * LANES, (t + 1) * LANES)
        gain = spread_scr[ex + 2 : ex + 3, at]
        gain_hi = gain.astype(BF).astype(F32)
        bc_rows = []
        for k in range(2):
            one = tails_bc[k][:, at]
            bc_rows.append(jnp.sum(jnp.where(row16 == s, one, 0.0), axis=0, keepdims=True))
        for half in range(2):
            values = [gain_hi, gain - gain_hi]
            for k in range(2):
                one = tails_x[k][:, at]
                values += [one[0:1], one[1:2]] if half == 0 else [one[2:3], bc_rows[k]]
            piece_ref[2 * t + half, 128:144, :] = as_rows(values).astype(BF)


def stage_b(xc_ref, bcc_ref, cum_ref, step_ref, fl_ref, skip_ref, y_ref):
    c = pl.program_id(0)
    row = lax.broadcasted_iota(I32, (STRETCH, LANES), 0)
    lane = lax.broadcasted_iota(I32, (STRETCH, LANES), 1)
    keep = (lane <= row) & (lane + c * STRETCH >= fl_ref[...])
    cum = cum_ref[...]
    cum_t = cum.T
    step_t = step_ref[...].T
    low = lax.broadcasted_iota(I32, (STRETCH, LANES), 1) < HEAD_DIM
    for g in range(GROUPS):
        b = bcc_ref[:, g * LANES : (g + 1) * LANES]
        cc = bcc_ref[:, (GROUPS + g) * LANES : (GROUPS + g + 1) * LANES]
        scores = lax.dot_general(cc, b, (((1,), (1,)), ((), ())), preferred_element_type=F32)
        for i in range(HEADS // GROUPS // 2):
            pair = g * (HEADS // GROUPS // 2) + i
            weights = []
            for h in (2 * pair, 2 * pair + 1):
                decay = jnp.exp(jnp.where(keep, cum[:, h : h + 1] - cum_t[h : h + 1, :], -jnp.inf))
                weights.append((scores * (decay * step_t[h : h + 1, :])).astype(BF))
            at = slice(pair * LANES, (pair + 1) * LANES)
            x = xc_ref[:, at]
            xf = x.astype(F32)
            both = jnp.concatenate(
                [jnp.where(low, xf, 0.0).astype(BF), jnp.where(low, 0.0, xf).astype(BF)], axis=0
            )
            inner = jnp.dot(
                jnp.concatenate(weights, axis=1), both, preferred_element_type=F32
            )
            y_ref[:, at] = inner + skip_ref[:, at] * xf


def stage_c(
    y_ref, z_ref, c_ref, ent_ref, s1_ref, s2_ref, entry_ref, cum_ref, fl_ref, gain_ref, out_ref
):
    g, c = pl.program_id(0), pl.program_id(1)
    lane = lax.broadcasted_iota(I32, (STRETCH, LANES), 1)
    inflow = jnp.where(fl_ref[...] < c * STRETCH, jnp.exp(cum_ref[...]), 0.0)
    wide = jnp.dot(
        split3(inflow, lane),
        spread_matrix(g * (HEADS // GROUPS), GWIDTH),
        preferred_element_type=F32,
    )
    incoming = s1_ref[...].astype(F32) + s2_ref[...].astype(F32)
    entering = ent_ref[0].astype(F32) + entry_ref[pl.ds(NC + c, 1), :] * incoming
    carried = jnp.dot(c_ref[...], entering.astype(BF), preferred_element_type=F32)
    gated = (y_ref[...] + wide * carried) * swish(z_ref[...].astype(F32))
    mean = jnp.sum(gated * gated, axis=1, keepdims=True) * (1.0 / GWIDTH)
    out_ref[...] = (gated * lax.rsqrt(mean + EPS) * gain_ref[...]).astype(BF)


def add_incoming(piece_ref, s1_ref, gain_ref, out_ref):
    for j in range(out_ref.shape[0]):
        at = slice((j // 2) * LANES, (j // 2 + 1) * LANES)
        came = s1_ref[(j % 2) * 64 : (j % 2) * 64 + 64, at].astype(F32)
        out_ref[j] = (piece_ref[j].astype(F32) + gain_ref[0:1, at] * came).astype(BF)


def pass_on(s1_ref, entry_ref, out_ref):
    out_ref[...] = (entry_ref[8:9, :] * s1_ref[...].astype(F32)).astype(BF)


def combine(len_ref, owner_ref, got_ref, out_ref):
    row16 = lax.broadcasted_iota(I32, (16, LANES), 0)

    def one(r, carry):
        first, before = carry
        last = first + len_ref[0, r] - 1
        home = last >> 9
        second = before == home
        h1 = jnp.maximum(home - 1, 0)
        slot = owner_ref[0, r]
        extra = got_ref[home, 128:144, :].astype(F32)
        gain = jnp.where(second, 0.0, extra[0:1] + extra[1:2])
        k = pl.multiple_of(jnp.where(second, 64, 0), 64)
        own = got_ref[home, pl.ds(k, 64), :].astype(F32)
        out_ref[slot, 0:64, :] = (own + gain * got_ref[h1, 0:64, :].astype(F32)).astype(BF)
        tail = jnp.where(second, pltpu.roll(extra, 12, 0), pltpu.roll(extra, 14, 0))
        out_ref[slot, 64:80, :] = jnp.where(row16 < 2, tail, 0.0).astype(BF)
        return last + 1, home

    lax.fori_loop(0, REQS, one, (jnp.int32(0), jnp.int32(-1)), unroll=2)


def finish(got_ref, state_ref, tx_ref, tbc_ref):
    tails = [got_ref[j, 64:80, :].astype(F32) for j in range(REQS)]
    for t in range(WIDTH // LANES):
        at = slice(t * LANES, (t + 1) * LANES)
        block = jnp.concatenate(
            [got_ref[2 * t, 0:64, :], got_ref[2 * t + 1, 0:64, :]], axis=0
        ).astype(F32)
        turned = block.T
        state_ref[2 * t] = turned[0:64]
        state_ref[2 * t + 1] = turned[64:128]
        tx_ref[:, at] = jnp.concatenate([tails[2 * t][0:2], tails[2 * t + 1][0:1]], axis=0).astype(BF)
    for k in range(KW - 1):
        for q in range(4):
            value = tails[2 * (4 * k + q) + 1][1:2].astype(BF)
            tbc_ref[k, q // 2 : q // 2 + 1, (q % 2) * LANES : (q % 2 + 1) * LANES] = value


def call(kernel, grid, ins, outs, scratch=(), flops=0, nbytes=0, aliases=None, limit=None):
    return pl.pallas_call(
        kernel,
        grid=grid,
        in_specs=ins,
        out_specs=[o[1] for o in outs],
        out_shape=[o[0] for o in outs],
        scratch_shapes=list(scratch),
        input_output_aliases=aliases or {},
        compiler_params=pltpu.CompilerParams(vmem_limit_bytes=limit or LARGE),
        cost_estimate=pl.CostEstimate(flops=flops, bytes_accessed=nbytes, transcendentals=0),
    )


def whole(*shape):
    return pl.BlockSpec(shape, lambda *_: (0,) * len(shape))


def on_device(
    x_in, bc_in, z_in, dt_in, conv_x_w, conv_x_b, conv_bc_w, conv_bc_b, a_log, dt_bias, skip_d,
    norm_gain, lengths, owner_slot,
):
    x = x_in[0]
    bc = bc_in[0].reshape(TOK, BCW)
    z = z_in[0]
    index = lax.axis_index("ctx").astype(I32).reshape(1)
    smem = pl.BlockSpec(memory_space=pltpu.SMEM)
    shape = jax.ShapeDtypeStruct
    cols = lambda rows: pl.BlockSpec((rows, SW), lambda s: (0, s))
    ends = bc_in[0, TOK - HALO :].reshape(HALO, BCW)
    halo = shift_in(jnp.concatenate([x[TOK - HALO :], ends], axis=1), 1)
    halo_cols = pl.BlockSpec((HALO, BCW), lambda s: (0, WIDTH // BCW))

    vmem = pl.BlockSpec(memory_space=pltpu.VMEM)
    by_head = shape((TOK, LANES), F32)
    cum, step, fl, wst = call(
        stage_p,
        (),
        [smem, smem, vmem, vmem, vmem],
        [
            (by_head, vmem),
            (by_head, vmem),
            (shape((TOK, LANES), I32), vmem),
            (shape((TOK + 16, LANES), BF), vmem),
        ],
        [pltpu.SMEM((REQS,), I32)],
        flops=10**8,
        nbytes=2**20,
    )(index, lengths, dt_in[0].T, a_log.reshape(1, HEADS), dt_bias.reshape(1, HEADS))

    xc, bcc, ent, left, entry = call(
        stage_a,
        (STEPS,),
        [
            cols(TOK),
            cols(HALO),
            whole(TOK, BCW),
            halo_cols,
            cols(KW),
            cols(1),
            whole(KW, 2, 2 * LANES),
            whole(2, 2 * LANES),
            whole(TOK, LANES),
            whole(TOK + 16, LANES),
        ],
        [
            (shape((TOK, WIDTH), BF), cols(TOK)),
            (shape((TOK, BCW), BF), whole(TOK, BCW)),
            (
                shape((NC, STATE, WIDTH), BF),
                pl.BlockSpec((NC, STATE, SW), lambda s: (0, 0, s)),
            ),
            (shape((STATE, WIDTH), BF), cols(STATE)),
            (shape((16, WIDTH), F32), cols(16)),
        ],
        [
            pltpu.VMEM((KW - 1, TOK, LANES), F32),
            pltpu.VMEM((TOK + 16, SW), F32),
            pltpu.VMEM((GROUPS * NC, STATE, STRETCH), BF),
        ],
        flops=10**9,
        nbytes=10 * 2**20,
    )(
        x, halo, bc, halo, conv_x_w, conv_x_b.reshape(1, WIDTH), conv_bc_w, conv_bc_b, fl, wst
    )

    s1 = shift_in(left, 1)

    pieces, gain = call(
        stage_e,
        (STEPS,),
        [
            smem,
            smem,
            cols(TOK),
            cols(HALO),
            whole(TOK, BCW),
            halo_cols,
            cols(TOK),
            whole(TOK, BCW),
            whole(TOK, LANES),
            whole(TOK, LANES),
            pl.BlockSpec((NC, STATE, SW), lambda s: (0, 0, s)),
            cols(STATE),
        ],
        [
            (
                shape((32, PIECE, LANES), BF),
                pl.BlockSpec((2 * SLT, PIECE, LANES), lambda s: (s, 0, 0)),
            ),
            (shape((8, WIDTH), F32), cols(8)),
        ],
        [
            pltpu.VMEM((2 * STRETCH + 16, LANES), BF),
            pltpu.VMEM((2 * STRETCH + 16, SW), F32),
            pltpu.SMEM((5,), I32),
        ],
        flops=5 * 10**8,
        nbytes=8 * 2**20,
    )(index, lengths, x, halo, bc, halo, xc, bcc, cum, step, ent, left)

    by_row = lambda width: pl.BlockSpec((STRETCH, width), lambda c: (c, 0))
    (y,) = call(
        stage_b,
        (NC,),
        [by_row(WIDTH), by_row(BCW), by_row(LANES), by_row(LANES), by_row(LANES), whole(1, WIDTH)],
        [(shape((TOK, WIDTH), F32), by_row(WIDTH))],
        flops=10**9,
        nbytes=20 * 2**20,
    )(xc, bcc, cum, step, fl, jnp.repeat(skip_d, HEAD_DIM).reshape(1, WIDTH))

    part = pl.BlockSpec((16, 64, LANES), lambda s: (s, 0, 0))
    half = lambda rows: pl.BlockSpec((rows, GWIDTH), lambda s: (0, s))
    (pieces,) = call(
        add_incoming,
        (2,),
        [part, half(STATE), half(8)],
        [(shape((32, PIECE, LANES), BF), part)],
        flops=10**7,
        nbytes=2 * 2**20,
        aliases={0: 0},
    )(pieces, s1, gain)
    got = lax.all_to_all(pieces, "ctx", split_axis=0, concat_axis=0, tiled=True)

    (passed,) = call(
        pass_on,
        (2,),
        [half(STATE), half(16)],
        [(shape((STATE, WIDTH), BF), half(STATE))],
        flops=10**7,
        nbytes=2 * 2**20,
        limit=SMALL,
    )(s1, entry)
    s2 = shift_in(passed, 1)

    got, s2, y = lax.optimization_barrier((got, s2, y))
    (back,) = call(
        combine,
        (),
        [smem, smem, pl.BlockSpec(memory_space=pltpu.VMEM)],
        [(shape((REQS, BACK, LANES), BF), pl.BlockSpec(memory_space=pltpu.VMEM))],
        flops=10**7,
        nbytes=3 * 2**20,
        limit=SMALL,
    )(lengths, owner_slot, got)
    own = lax.all_to_all(back, "ctx", split_axis=0, concat_axis=0, tiled=True)

    back, y = lax.optimization_barrier((back, y))
    by_c = lambda g, c: (c, 0)
    by_g = lambda g, c: (0, g)
    by_cg = lambda g, c: (c, g)
    (mixed,) = call(
        stage_c,
        (GROUPS, NC),
        [
            pl.BlockSpec((STRETCH, GWIDTH), by_cg),
            pl.BlockSpec((STRETCH, GWIDTH), by_cg),
            pl.BlockSpec((STRETCH, LANES), lambda g, c: (c, GROUPS + g)),
            pl.BlockSpec((1, STATE, GWIDTH), lambda g, c: (c, 0, g)),
            pl.BlockSpec((STATE, GWIDTH), by_g),
            pl.BlockSpec((STATE, GWIDTH), by_g),
            pl.BlockSpec((16, GWIDTH), by_g),
            pl.BlockSpec((STRETCH, LANES), by_c),
            pl.BlockSpec((STRETCH, LANES), by_c),
            pl.BlockSpec((1, GWIDTH), by_g),
        ],
        [(shape((TOK, WIDTH), BF), pl.BlockSpec((STRETCH, GWIDTH), by_cg))],
        flops=10**9,
        nbytes=15 * 2**20,
    )(y, z, bcc, ent, s1, s2, entry, cum, fl, norm_gain.reshape(1, WIDTH))

    own, mixed = lax.optimization_barrier((own, mixed))
    swapped = lax.ppermute(own, "side", [(0, 1), (1, 0)])
    state, tail_x, tail_bc = call(
        finish,
        (),
        [pl.BlockSpec(memory_space=pltpu.VMEM)],
        [
            (shape((HEADS, HEAD_DIM, STATE), F32), pl.BlockSpec(memory_space=pltpu.VMEM)),
            (shape((KW - 1, WIDTH), BF), pl.BlockSpec(memory_space=pltpu.VMEM)),
            (shape((KW - 1, 2, 2 * LANES), BF), pl.BlockSpec(memory_space=pltpu.VMEM)),
        ],
        flops=10**7,
        nbytes=3 * 2**20,
        limit=SMALL,
    )(swapped)
    return mixed[None], state[None, None], tail_x[None, None], tail_bc[None, None]


def solution(mesh):
    placed = (
        P("side", "ctx", "head"),
        P("side", "ctx", None, "head"),
        P("side", "ctx", "head"),
        P("side", "ctx", "head"),
        P(None, "head"),
        P("head"),
        P(None, None, "head"),
        P(None, "head"),
        P("head"),
        P("head"),
        P("head"),
        P("head"),
        P("side", None),
        P("side", None),
    )
    return jax.shard_map(
        on_device,
        mesh=mesh,
        in_specs=placed,
        out_specs=(
            P("side", "ctx", "head"),
            P("side", "ctx", "head", None, None),
            P("side", "ctx", None, "head"),
            P("side", "ctx", None, None, "head"),
        ),
        check_vma=False,
    )
```

```python
import jax
import jax.numpy as jnp
from jax import lax
from jax.experimental import pallas as pl
from jax.experimental.pallas import tpu as pltpu
from jax.sharding import PartitionSpec as P

HEAD_DIM = 64
STATE = 128
STRETCH = 128
LANES = 128
HALO = 16
KW = 4
EPS = 1e-05
BF = jnp.bfloat16
F32 = jnp.float32
I32 = jnp.int32
LARGE = 60 * 1024 * 1024
SMALL = 16 * 1024 * 1024

TOK = 512
NC = TOK // STRETCH
WIDTH = 2048
HEADS = WIDTH // HEAD_DIM
GROUPS = 2
GWIDTH = WIDTH // GROUPS
BCW = 512
REQS = 32
STEPS = 4
SW = WIDTH // STEPS
SLT = SW // LANES
PIECE = 2 * 64 + 8
BACK = 64 + 8


def shift_in(block, distance):
    count = lax.axis_size("ctx")
    return lax.ppermute(block, "ctx", [(i, i + distance) for i in range(count - distance)])


def swish(v):
    half = 0.5 * v
    return half + half * jnp.tanh(half)


def split3(v, lane):
    hi = v.astype(BF).astype(F32)
    rest = v - hi
    mid = rest.astype(BF).astype(F32)
    low = rest - mid
    return jnp.where(
        lane < HEADS, hi, jnp.where(lane < 2 * HEADS, mid, jnp.where(lane < 3 * HEADS, low, 0.0))
    ).astype(BF)


def spread_matrix(first_head, width):
    row = lax.broadcasted_iota(I32, (LANES, width), 0)
    col = lax.broadcasted_iota(I32, (LANES, width), 1)
    same = ((row & (HEADS - 1)) == (col >> 6) + first_head) & (row < 3 * HEADS)
    return jnp.where(same, 1.0, 0.0).astype(BF)


def conv_tile(ext, taps, bias, masks):
    acc = bias + taps[KW - 1] * ext[HALO:]
    for d in range(1, KW):
        acc = acc + taps[KW - 1 - d] * (pltpu.roll(ext, d, 0)[HALO:] * masks[d - 1])
    return swish(acc)


def scan_lengths(idx_ref, len_ref):
    zero = jnp.int32(0)

    def scan(r, carry):
        first, count, behind, e0, f0, e1, f1, fa = carry
        last = first + len_ref[0, r] - 1
        ends = (last >= 0) & (last < TOK)
        take0, take1 = ends & (count == 0), ends & (count == 1)
        points = [c * STRETCH + STRETCH - 1 for c in range(NC)]
        fa = tuple(
            jnp.where((first <= p) & (last >= p), first, old) for p, old in zip(points, fa)
        )
        return (
            last + 1,
            count + jnp.where(ends, 1, 0),
            behind + jnp.where((last >= -TOK) & (last < 0), 1, 0),
            jnp.where(take0, last, e0),
            jnp.where(take0, first, f0),
            jnp.where(take1, last, e1),
            jnp.where(take1, first, f1),
            fa,
        )

    start = -idx_ref[0] * TOK
    out = lax.fori_loop(
        0, REQS, scan, (start, zero, zero, zero, zero, zero, zero, (zero,) * NC), unroll=4
    )
    return out[1:]


def stretch_gains(cum_ref, fa):
    through = []
    gains = [jnp.ones((1, LANES), F32)]
    for c in range(NC):
        end = cum_ref[(c + 1) * STRETCH - 1 : (c + 1) * STRETCH, :]
        through.append(jnp.where(fa[c] < c * STRETCH, jnp.exp(end), 0.0))
        gains.append(gains[-1] * through[-1])
    return through, gains


def as_rows(values):
    row16 = lax.broadcasted_iota(I32, (16, LANES), 0)
    block = jnp.zeros((16, LANES), F32)
    for i, v in enumerate(values):
        block = jnp.where(row16 == i, v, block)
    return block


def stage_p(
    idx_ref, len_ref, dt_ref, al_ref, db_ref, cum_ref, step_ref, fl_ref, wst_ref
):
    lane = lax.broadcasted_iota(I32, (STRETCH, LANES), 1)
    row = lax.broadcasted_iota(I32, (STRETCH, LANES), 0)
    lane_f = lane.astype(F32)
    start = (-idx_ref[0] * TOK).astype(F32)
    lengths = jnp.concatenate([len_ref[...].astype(F32)] * 4, axis=1)
    earlier = jnp.where((row < lane) & (row < REQS), 1.0, 0.0)
    first = start + jnp.dot(
        jnp.broadcast_to(lengths, (8, LANES)),
        earlier,
        precision=lax.Precision.HIGHEST,
        preferred_element_type=F32,
    )[0:1, :]
    first = jnp.where(lane_f[0:1, :] < REQS, first, start)
    coef = -jnp.exp(jnp.concatenate([al_ref[...]] * 4, axis=1))
    bias = jnp.concatenate([db_ref[...]] * 4, axis=1)
    lower = jnp.where(row >= lane, 1.0, 0.0)
    through = []
    gains = [jnp.ones((1, LANES), F32)]
    for c in range(NC):
        rows = slice(c * STRETCH, (c + 1) * STRETCH)
        here = row + c * STRETCH
        started = jnp.where(first <= here.astype(F32), first, start)
        fl = jnp.broadcast_to(jnp.max(started, axis=1, keepdims=True), (STRETCH, LANES))
        fl = fl.astype(I32)
        fl_ref[rows, :] = fl
        raw = jnp.concatenate([dt_ref[:, rows]] * 4, axis=0).T + bias
        step = jnp.maximum(raw, 0.0) + jnp.log1p(jnp.exp(-jnp.abs(raw)))
        step_ref[rows, :] = step
        cum = jnp.dot(
            lower, coef * step, precision=lax.Precision.HIGHEST, preferred_element_type=F32
        )
        cum_ref[rows, :] = cum
        end, fa = cum[STRETCH - 1 :, :], fl[STRETCH - 1 :, :]
        w = jnp.exp(end - cum) * step
        wst_ref[rows, :] = split3(jnp.where(here >= fa, w, 0.0), lane)
        through.append(jnp.where(fa < c * STRETCH, jnp.exp(end), 0.0))
        gains.append(gains[-1] * through[-1])
    lane16 = lax.broadcasted_iota(I32, (16, LANES), 1)
    wst_ref[NC * STRETCH :, :] = split3(as_rows(through + gains), lane16)


def stage_a(
    x_ref, xh_ref, bc_ref, bch_ref, wx_ref, bx_ref, wbc_ref, bbc_ref, fl_ref, wst_ref,
    xc_ref, bcc_ref, ent_ref, s_ref, entry_ref,
    mask_scr, spread_scr, bt_scr,
):
    s = pl.program_id(0)
    row = lax.broadcasted_iota(I32, (STRETCH, LANES), 0)

    @pl.when(s == 0)
    def _():
        for c in range(NC):
            rows = slice(c * STRETCH, (c + 1) * STRETCH)
            since = row + c * STRETCH - fl_ref[rows, :]
            for d in range(1, KW):
                mask_scr[d - 1, rows, :] = jnp.where(since >= d, 1.0, 0.0)
        for part in range(2):
            for g in range(GROUPS):
                at = slice((part * GROUPS + g) * LANES, (part * GROUPS + g + 1) * LANES)
                own = slice(g * LANES, (g + 1) * LANES)
                taps = [wbc_ref[k, part : part + 1, own] for k in range(KW)]
                off = bbc_ref[part : part + 1, own]
                for c in range(NC):
                    if c == 0:
                        ext = jnp.concatenate([bch_ref[:, at], bc_ref[0:STRETCH, at]], axis=0)
                    else:
                        ext = bc_ref[c * STRETCH - HALO : (c + 1) * STRETCH, at]
                    rows = slice(c * STRETCH, (c + 1) * STRETCH)
                    masks = [mask_scr[d, rows, :] for d in range(KW - 1)]
                    out = conv_tile(ext.astype(F32), taps, off, masks).astype(BF)
                    bcc_ref[rows, at] = out
                    if part == 0:
                        bt_scr[g * NC + c] = out.astype(F32).T.astype(BF)

    spread_scr[...] = jnp.dot(
        wst_ref[...], spread_matrix(s * (SW // HEAD_DIM), SW), preferred_element_type=F32
    )
    ex = NC * STRETCH
    group = s // (STEPS // GROUPS)
    entry_ref[...] = spread_scr[ex:, :]
    entering = None
    for c in range(NC):
        rows = slice(c * STRETCH, (c + 1) * STRETCH)
        masks = [mask_scr[d, rows, :] for d in range(KW - 1)]
        scaled = []
        for t in range(SLT):
            at = slice(t * LANES, (t + 1) * LANES)
            if c == 0:
                ext = jnp.concatenate([xh_ref[:, at], x_ref[0:STRETCH, at]], axis=0)
            else:
                ext = x_ref[c * STRETCH - HALO : (c + 1) * STRETCH, at]
            taps = [wx_ref[k : k + 1, at] for k in range(KW)]
            out = conv_tile(ext.astype(F32), taps, bx_ref[:, at], masks).astype(BF)
            xc_ref[rows, at] = out
            scaled.append((out.astype(F32) * spread_scr[rows, at]).astype(BF))
        local = jnp.dot(
            bt_scr[group * NC + c], jnp.concatenate(scaled, axis=1), preferred_element_type=F32
        )
        if c == 0:
            ent_ref[0] = jnp.zeros((STATE, SW), BF)
            entering = local
        else:
            ent_ref[c] = entering.astype(BF)
            entering = spread_scr[ex + c : ex + c + 1, :] * entering + local
    s_ref[...] = entering.astype(BF)


def stage_e(
    idx_ref, len_ref, x_ref, xh_ref, bc_ref, bch_ref, xc_ref, bcc_ref, cum_ref, step_ref, ent_ref,
    s_ref,
    piece_ref, gain_ref,
    wst_scr, spread_scr, sc_scr,
):
    s = pl.program_id(0)
    lane = lax.broadcasted_iota(I32, (STRETCH, LANES), 1)
    row = lax.broadcasted_iota(I32, (STRETCH, LANES), 0)
    ex = 2 * STRETCH

    @pl.when(s == 0)
    def _():
        count, behind, e0, f0, e1, f1, fa = scan_lengths(idx_ref, len_ref)
        sc_scr[0], sc_scr[1], sc_scr[2], sc_scr[3], sc_scr[4] = e0, f0, e1, f1, count
        inflow = []
        for k, (e, f) in enumerate(((e0, f0), (e1, f1))):
            base = pl.multiple_of((e >> 7) * STRETCH, STRETCH)
            here = row + base
            end = cum_ref[pl.ds(e, 1), :]
            w = jnp.exp(end - cum_ref[pl.ds(base, STRETCH), :]) * step_ref[pl.ds(base, STRETCH), :]
            w = jnp.where((here >= f) & (here <= e), w, 0.0)
            wst_scr[k * STRETCH : (k + 1) * STRETCH, :] = split3(w, lane)
            inflow.append(jnp.where(f < base, jnp.exp(end), 0.0))
        _, gains = stretch_gains(cum_ref, fa)
        gain = gains[0]
        for c in range(1, NC):
            gain = jnp.where((e0 >> 7) == c, gains[c], gain)
        gain = gain * inflow[0]
        by_owner = jnp.where((count > 0) & (behind == 0), gain, 0.0)
        by_sender = jnp.where(count == 0, gains[NC], jnp.where(behind == 0, 0.0, gain))
        lane16 = lax.broadcasted_iota(I32, (16, LANES), 1)
        wst_scr[ex:, :] = split3(as_rows(inflow + [by_owner, by_sender]), lane16)

    e0, f0, e1, f1 = sc_scr[0], sc_scr[1], sc_scr[2], sc_scr[3]
    spread_scr[...] = jnp.dot(
        wst_scr[...], spread_matrix(s * (SW // HEAD_DIM), SW), preferred_element_type=F32
    )
    gain_ref[...] = jnp.broadcast_to(spread_scr[ex + 3 : ex + 4, :], (8, SW))
    group = s // (STEPS // GROUPS)
    for k, e in enumerate((e0, e1)):
        c = e >> 7
        base = pl.multiple_of(c * STRETCH, STRETCH)
        at = k * STRETCH
        scaled = (
            xc_ref[pl.ds(base, STRETCH), :].astype(F32) * spread_scr[at : at + STRETCH, :]
        ).astype(BF)
        b = jnp.where(
            group == 0,
            bcc_ref[pl.ds(base, STRETCH), 0:LANES].astype(F32),
            bcc_ref[pl.ds(base, STRETCH), LANES : 2 * LANES].astype(F32),
        )
        final = spread_scr[ex + k : ex + k + 1, :] * ent_ref[c].astype(F32) + jnp.dot(
            b.T.astype(BF), scaled, preferred_element_type=F32
        )
        if k == 0:
            final = jnp.where(sc_scr[4] == 0, s_ref[...].astype(F32), final)
        final = final.astype(BF)
        for j in range(2 * SLT):
            piece_ref[j, k * 64 : k * 64 + 64, :] = final[
                (j % 2) * 64 : (j % 2) * 64 + 64, (j // 2) * LANES : (j // 2 + 1) * LANES
            ]

    tails_x, tails_bc = [], []
    pick_row = lax.broadcasted_iota(I32, (16, 2 * HALO), 0)
    pick_col = lax.broadcasted_iota(I32, (16, 2 * HALO), 1)
    for e, f in ((e0, f0), (e1, f1)):
        base = pl.multiple_of((e >> 4) * HALO, HALO)
        before = pl.multiple_of(jnp.maximum(base - HALO, 0), HALO)
        source = e - (KW - 2) + pick_row
        pick = (pick_col + base - HALO == source) & (source >= f) & (pick_row < KW - 1)
        pick = jnp.where(pick, 1.0, 0.0).astype(BF)

        def tail(ref, halo_ref):
            head = jnp.where(base > 0, ref[pl.ds(before, HALO), :], halo_ref[...])
            window = jnp.concatenate([head, ref[pl.ds(base, HALO), :]], axis=0)
            return jnp.dot(pick, window, preferred_element_type=F32)

        tails_x.append(tail(x_ref, xh_ref))
        tails_bc.append(tail(bc_ref, bch_ref))
    row16 = lax.broadcasted_iota(I32, (16, LANES), 0)
    for t in range(SLT):
        at = slice(t * LANES, (t + 1) * LANES)
        gain = spread_scr[ex + 2 : ex + 3, at]
        gain_hi = gain.astype(BF).astype(F32)
        bc_rows = []
        for k in range(2):
            one = tails_bc[k][:, at]
            bc_rows.append(jnp.sum(jnp.where(row16 == s, one, 0.0), axis=0, keepdims=True))
        for half in range(2):
            values = [gain_hi, gain - gain_hi]
            for k in range(2):
                one = tails_x[k][:, at]
                values += [one[0:1], one[1:2]] if half == 0 else [one[2:3], bc_rows[k]]
            piece_ref[2 * t + half, 128:136, :] = as_rows(values)[0:8].astype(BF)


def stage_b(xc_ref, bcc_ref, cum_ref, step_ref, fl_ref, skip_ref, y_ref):
    c = pl.program_id(0)
    row = lax.broadcasted_iota(I32, (STRETCH, LANES), 0)
    lane = lax.broadcasted_iota(I32, (STRETCH, LANES), 1)
    keep = (lane <= row) & (lane + c * STRETCH >= fl_ref[...])
    cum = cum_ref[...]
    cum_t = cum.T
    step_t = step_ref[...].T
    low = lax.broadcasted_iota(I32, (STRETCH, LANES), 1) < HEAD_DIM
    for g in range(GROUPS):
        b = bcc_ref[:, g * LANES : (g + 1) * LANES]
        cc = bcc_ref[:, (GROUPS + g) * LANES : (GROUPS + g + 1) * LANES]
        scores = lax.dot_general(cc, b, (((1,), (1,)), ((), ())), preferred_element_type=F32)
        for i in range(HEADS // GROUPS // 2):
            pair = g * (HEADS // GROUPS // 2) + i
            weights = []
            for h in (2 * pair, 2 * pair + 1):
                decay = jnp.exp(jnp.where(keep, cum[:, h : h + 1] - cum_t[h : h + 1, :], -jnp.inf))
                weights.append((scores * (decay * step_t[h : h + 1, :])).astype(BF))
            at = slice(pair * LANES, (pair + 1) * LANES)
            x = xc_ref[:, at]
            xf = x.astype(F32)
            both = jnp.concatenate(
                [jnp.where(low, xf, 0.0).astype(BF), jnp.where(low, 0.0, xf).astype(BF)], axis=0
            )
            inner = jnp.dot(
                jnp.concatenate(weights, axis=1), both, preferred_element_type=F32
            )
            y_ref[:, at] = inner + skip_ref[:, at] * xf


def stage_c(
    y_ref, z_ref, c_ref, ent_ref, s1_ref, s2_ref, entry_ref, cum_ref, fl_ref, gain_ref, out_ref
):
    g, c = pl.program_id(0), pl.program_id(1)
    lane = lax.broadcasted_iota(I32, (STRETCH, LANES), 1)
    inflow = jnp.where(fl_ref[...] < c * STRETCH, jnp.exp(cum_ref[...]), 0.0)
    wide = jnp.dot(
        split3(inflow, lane),
        spread_matrix(g * (HEADS // GROUPS), GWIDTH),
        preferred_element_type=F32,
    )
    incoming = s1_ref[...].astype(F32) + s2_ref[...].astype(F32)
    entering = ent_ref[0].astype(F32) + entry_ref[pl.ds(NC + c, 1), :] * incoming
    carried = jnp.dot(c_ref[...], entering.astype(BF), preferred_element_type=F32)
    gated = (y_ref[...] + wide * carried) * swish(z_ref[...].astype(F32))
    mean = jnp.sum(gated * gated, axis=1, keepdims=True) * (1.0 / GWIDTH)
    out_ref[...] = (gated * lax.rsqrt(mean + EPS) * gain_ref[...]).astype(BF)


def add_incoming(piece_ref, s1_ref, gain_ref, out_ref):
    for j in range(out_ref.shape[0]):
        at = slice((j // 2) * LANES, (j // 2 + 1) * LANES)
        came = s1_ref[(j % 2) * 64 : (j % 2) * 64 + 64, at].astype(F32)
        out_ref[j] = (piece_ref[j].astype(F32) + gain_ref[0:1, at] * came).astype(BF)


def pass_on(s1_ref, entry_ref, out_ref):
    out_ref[...] = (entry_ref[8:9, :] * s1_ref[...].astype(F32)).astype(BF)


def combine(len_ref, owner_ref, got_ref, out_ref):
    row8 = lax.broadcasted_iota(I32, (8, LANES), 0)

    def one(r, carry):
        first, before = carry
        last = first + len_ref[0, r] - 1
        home = last >> 9
        second = before == home
        h1 = jnp.maximum(home - 1, 0)
        slot = owner_ref[0, r]
        extra = got_ref[home, 128:136, :].astype(F32)
        gain = jnp.where(second, 0.0, extra[0:1] + extra[1:2])
        k = pl.multiple_of(jnp.where(second, 64, 0), 64)
        own = got_ref[home, pl.ds(k, 64), :].astype(F32)
        out_ref[slot, 0:64, :] = (own + gain * got_ref[h1, 0:64, :].astype(F32)).astype(BF)
        tail = jnp.where(second, pltpu.roll(extra, 4, 0), pltpu.roll(extra, 6, 0))
        out_ref[slot, 64:72, :] = jnp.where(row8 < 2, tail, 0.0).astype(BF)
        return last + 1, home

    lax.fori_loop(0, REQS, one, (jnp.int32(0), jnp.int32(-1)), unroll=2)


def finish(got_ref, state_ref, tx_ref, tbc_ref):
    tails = [got_ref[j, 64:72, :].astype(F32) for j in range(REQS)]
    for t in range(WIDTH // LANES):
        at = slice(t * LANES, (t + 1) * LANES)
        block = jnp.concatenate(
            [got_ref[2 * t, 0:64, :], got_ref[2 * t + 1, 0:64, :]], axis=0
        ).astype(F32)
        turned = block.T
        state_ref[2 * t] = turned[0:64]
        state_ref[2 * t + 1] = turned[64:128]
        tx_ref[:, at] = jnp.concatenate([tails[2 * t][0:2], tails[2 * t + 1][0:1]], axis=0).astype(BF)
    for k in range(KW - 1):
        for q in range(4):
            value = tails[2 * (4 * k + q) + 1][1:2].astype(BF)
            tbc_ref[k, q // 2 : q // 2 + 1, (q % 2) * LANES : (q % 2 + 1) * LANES] = value


def call(kernel, grid, ins, outs, scratch=(), flops=0, nbytes=0, aliases=None, limit=None):
    return pl.pallas_call(
        kernel,
        grid=grid,
        in_specs=ins,
        out_specs=[o[1] for o in outs],
        out_shape=[o[0] for o in outs],
        scratch_shapes=list(scratch),
        input_output_aliases=aliases or {},
        compiler_params=pltpu.CompilerParams(vmem_limit_bytes=limit or LARGE),
        cost_estimate=pl.CostEstimate(flops=flops, bytes_accessed=nbytes, transcendentals=0),
    )


def whole(*shape):
    return pl.BlockSpec(shape, lambda *_: (0,) * len(shape))


def on_device(
    x_in, bc_in, z_in, dt_in, conv_x_w, conv_x_b, conv_bc_w, conv_bc_b, a_log, dt_bias, skip_d,
    norm_gain, lengths, owner_slot,
):
    x = x_in[0]
    bc = bc_in[0].reshape(TOK, BCW)
    z = z_in[0]
    index = lax.axis_index("ctx").astype(I32).reshape(1)
    smem = pl.BlockSpec(memory_space=pltpu.SMEM)
    shape = jax.ShapeDtypeStruct
    cols = lambda rows: pl.BlockSpec((rows, SW), lambda s: (0, s))
    ends = bc_in[0, TOK - HALO :].reshape(HALO, BCW)
    halo = shift_in(jnp.concatenate([x[TOK - HALO :], ends], axis=1), 1)
    halo_cols = pl.BlockSpec((HALO, BCW), lambda s: (0, WIDTH // BCW))

    vmem = pl.BlockSpec(memory_space=pltpu.VMEM)
    by_head = shape((TOK, LANES), F32)
    cum, step, fl, wst = call(
        stage_p,
        (),
        [smem, vmem, vmem, vmem, vmem],
        [
            (by_head, vmem),
            (by_head, vmem),
            (shape((TOK, LANES), I32), vmem),
            (shape((TOK + 16, LANES), BF), vmem),
        ],
        flops=10**8,
        nbytes=2**20,
    )(index, lengths, dt_in[0].T, a_log.reshape(1, HEADS), dt_bias.reshape(1, HEADS))

    xc, bcc, ent, left, entry = call(
        stage_a,
        (STEPS,),
        [
            cols(TOK),
            cols(HALO),
            whole(TOK, BCW),
            halo_cols,
            cols(KW),
            cols(1),
            whole(KW, 2, 2 * LANES),
            whole(2, 2 * LANES),
            whole(TOK, LANES),
            whole(TOK + 16, LANES),
        ],
        [
            (shape((TOK, WIDTH), BF), cols(TOK)),
            (shape((TOK, BCW), BF), whole(TOK, BCW)),
            (
                shape((NC, STATE, WIDTH), BF),
                pl.BlockSpec((NC, STATE, SW), lambda s: (0, 0, s)),
            ),
            (shape((STATE, WIDTH), BF), cols(STATE)),
            (shape((16, WIDTH), F32), cols(16)),
        ],
        [
            pltpu.VMEM((KW - 1, TOK, LANES), F32),
            pltpu.VMEM((TOK + 16, SW), F32),
            pltpu.VMEM((GROUPS * NC, STATE, STRETCH), BF),
        ],
        flops=10**9,
        nbytes=10 * 2**20,
    )(
        x, halo, bc, halo, conv_x_w, conv_x_b.reshape(1, WIDTH), conv_bc_w, conv_bc_b, fl, wst
    )

    s1 = shift_in(left, 1)

    pieces, gain = call(
        stage_e,
        (STEPS,),
        [
            smem,
            smem,
            cols(TOK),
            cols(HALO),
            whole(TOK, BCW),
            halo_cols,
            cols(TOK),
            whole(TOK, BCW),
            whole(TOK, LANES),
            whole(TOK, LANES),
            pl.BlockSpec((NC, STATE, SW), lambda s: (0, 0, s)),
            cols(STATE),
        ],
        [
            (
                shape((32, PIECE, LANES), BF),
                pl.BlockSpec((2 * SLT, PIECE, LANES), lambda s: (s, 0, 0)),
            ),
            (shape((8, WIDTH), F32), cols(8)),
        ],
        [
            pltpu.VMEM((2 * STRETCH + 16, LANES), BF),
            pltpu.VMEM((2 * STRETCH + 16, SW), F32),
            pltpu.SMEM((5,), I32),
        ],
        flops=5 * 10**8,
        nbytes=8 * 2**20,
    )(index, lengths, x, halo, bc, halo, xc, bcc, cum, step, ent, left)

    by_row = lambda width: pl.BlockSpec((STRETCH, width), lambda c: (c, 0))
    (y,) = call(
        stage_b,
        (NC,),
        [by_row(WIDTH), by_row(BCW), by_row(LANES), by_row(LANES), by_row(LANES), whole(1, WIDTH)],
        [(shape((TOK, WIDTH), F32), by_row(WIDTH))],
        flops=10**9,
        nbytes=20 * 2**20,
    )(xc, bcc, cum, step, fl, jnp.repeat(skip_d, HEAD_DIM).reshape(1, WIDTH))

    part = pl.BlockSpec((16, 64, LANES), lambda s: (s, 0, 0))
    half = lambda rows: pl.BlockSpec((rows, GWIDTH), lambda s: (0, s))
    (pieces,) = call(
        add_incoming,
        (2,),
        [part, half(STATE), half(8)],
        [(shape((32, PIECE, LANES), BF), part)],
        flops=10**7,
        nbytes=2 * 2**20,
        aliases={0: 0},
    )(pieces, s1, gain)
    got = lax.all_to_all(pieces, "ctx", split_axis=0, concat_axis=0, tiled=True)

    (passed,) = call(
        pass_on,
        (2,),
        [half(STATE), half(16)],
        [(shape((STATE, WIDTH), BF), half(STATE))],
        flops=10**7,
        nbytes=2 * 2**20,
        limit=SMALL,
    )(s1, entry)
    s2 = shift_in(passed, 1)

    got, s2, y = lax.optimization_barrier((got, s2, y))
    (back,) = call(
        combine,
        (),
        [smem, smem, pl.BlockSpec(memory_space=pltpu.VMEM)],
        [(shape((REQS, BACK, LANES), BF), pl.BlockSpec(memory_space=pltpu.VMEM))],
        flops=10**7,
        nbytes=3 * 2**20,
        limit=SMALL,
    )(lengths, owner_slot, got)
    own = lax.all_to_all(back, "ctx", split_axis=0, concat_axis=0, tiled=True)

    back, y = lax.optimization_barrier((back, y))
    by_c = lambda g, c: (c, 0)
    by_g = lambda g, c: (0, g)
    by_cg = lambda g, c: (c, g)
    (mixed,) = call(
        stage_c,
        (GROUPS, NC),
        [
            pl.BlockSpec((STRETCH, GWIDTH), by_cg),
            pl.BlockSpec((STRETCH, GWIDTH), by_cg),
            pl.BlockSpec((STRETCH, LANES), lambda g, c: (c, GROUPS + g)),
            pl.BlockSpec((1, STATE, GWIDTH), lambda g, c: (c, 0, g)),
            pl.BlockSpec((STATE, GWIDTH), by_g),
            pl.BlockSpec((STATE, GWIDTH), by_g),
            pl.BlockSpec((16, GWIDTH), by_g),
            pl.BlockSpec((STRETCH, LANES), by_c),
            pl.BlockSpec((STRETCH, LANES), by_c),
            pl.BlockSpec((1, GWIDTH), by_g),
        ],
        [(shape((TOK, WIDTH), BF), pl.BlockSpec((STRETCH, GWIDTH), by_cg))],
        flops=10**9,
        nbytes=15 * 2**20,
    )(y, z, bcc, ent, s1, s2, entry, cum, fl, norm_gain.reshape(1, WIDTH))

    own, mixed = lax.optimization_barrier((own, mixed))
    swapped = lax.ppermute(own, "side", [(0, 1), (1, 0)])
    state, tail_x, tail_bc = call(
        finish,
        (),
        [pl.BlockSpec(memory_space=pltpu.VMEM)],
        [
            (shape((HEADS, HEAD_DIM, STATE), F32), pl.BlockSpec(memory_space=pltpu.VMEM)),
            (shape((KW - 1, WIDTH), BF), pl.BlockSpec(memory_space=pltpu.VMEM)),
            (shape((KW - 1, 2, 2 * LANES), BF), pl.BlockSpec(memory_space=pltpu.VMEM)),
        ],
        flops=10**7,
        nbytes=3 * 2**20,
        limit=SMALL,
    )(swapped)
    return mixed[None], state[None, None], tail_x[None, None], tail_bc[None, None]


def solution(mesh):
    placed = (
        P("side", "ctx", "head"),
        P("side", "ctx", None, "head"),
        P("side", "ctx", "head"),
        P("side", "ctx", "head"),
        P(None, "head"),
        P("head"),
        P(None, None, "head"),
        P(None, "head"),
        P("head"),
        P("head"),
        P("head"),
        P("head"),
        P("side", None),
        P("side", None),
    )
    return jax.shard_map(
        on_device,
        mesh=mesh,
        in_specs=placed,
        out_specs=(
            P("side", "ctx", "head"),
            P("side", "ctx", "head", None, None),
            P("side", "ctx", None, "head"),
            P("side", "ctx", None, None, "head"),
        ),
        check_vma=False,
    )
```

```python
import jax
import jax.numpy as jnp
from jax import lax
from jax.experimental import pallas as pl
from jax.experimental.pallas import tpu as pltpu
from jax.sharding import PartitionSpec as P

HEAD_DIM = 64
STATE = 128
STRETCH = 128
LANES = 128
HALO = 16
KW = 4
EPS = 1e-05
BF = jnp.bfloat16
F32 = jnp.float32
I32 = jnp.int32
LARGE = 60 * 1024 * 1024
SMALL = 16 * 1024 * 1024

TOK = 512
NC = TOK // STRETCH
WIDTH = 2048
HEADS = WIDTH // HEAD_DIM
GROUPS = 2
GWIDTH = WIDTH // GROUPS
BCW = 512
REQS = 32
ROW_Y = 4
STEPS = 4
SW = WIDTH // STEPS
SLT = SW // LANES
PIECE = 2 * 64 + 8
BACK = 64 + 8


def shift_in(block, distance):
    count = lax.axis_size("ctx")
    return lax.ppermute(block, "ctx", [(i, i + distance) for i in range(count - distance)])


def shift_pairs(block, distance, keep):
    count = lax.axis_size("ctx")
    pairs = [(i, i + distance) for i in range(count - distance) if i % ROW_Y in keep]
    return lax.ppermute(block, "ctx", pairs)


def swish(v):
    half = 0.5 * v
    return half + half * jnp.tanh(half)


def split3(v, lane):
    hi = v.astype(BF).astype(F32)
    rest = v - hi
    mid = rest.astype(BF).astype(F32)
    low = rest - mid
    return jnp.where(
        lane < HEADS, hi, jnp.where(lane < 2 * HEADS, mid, jnp.where(lane < 3 * HEADS, low, 0.0))
    ).astype(BF)


def spread_matrix(first_head, width):
    row = lax.broadcasted_iota(I32, (LANES, width), 0)
    col = lax.broadcasted_iota(I32, (LANES, width), 1)
    same = ((row & (HEADS - 1)) == (col >> 6) + first_head) & (row < 3 * HEADS)
    return jnp.where(same, 1.0, 0.0).astype(BF)


def conv_tile(ext, taps, bias, masks):
    acc = bias + taps[KW - 1] * ext[HALO:]
    for d in range(1, KW):
        acc = acc + taps[KW - 1 - d] * (pltpu.roll(ext, d, 0)[HALO:] * masks[d - 1])
    return swish(acc)


def scan_lengths(idx_ref, len_ref):
    zero = jnp.int32(0)

    def scan(r, carry):
        first, count, behind, e0, f0, e1, f1, fa = carry
        last = first + len_ref[0, r] - 1
        ends = (last >= 0) & (last < TOK)
        take0, take1 = ends & (count == 0), ends & (count == 1)
        points = [c * STRETCH + STRETCH - 1 for c in range(NC)]
        fa = tuple(
            jnp.where((first <= p) & (last >= p), first, old) for p, old in zip(points, fa)
        )
        return (
            last + 1,
            count + jnp.where(ends, 1, 0),
            behind + jnp.where((last >= -TOK) & (last < 0), 1, 0),
            jnp.where(take0, last, e0),
            jnp.where(take0, first, f0),
            jnp.where(take1, last, e1),
            jnp.where(take1, first, f1),
            fa,
        )

    start = -idx_ref[0] * TOK
    out = lax.fori_loop(
        0, REQS, scan, (start, zero, zero, zero, zero, zero, zero, (zero,) * NC), unroll=4
    )
    return out[1:]


def stretch_gains(cum_ref, fa):
    through = []
    gains = [jnp.ones((1, LANES), F32)]
    for c in range(NC):
        end = cum_ref[(c + 1) * STRETCH - 1 : (c + 1) * STRETCH, :]
        through.append(jnp.where(fa[c] < c * STRETCH, jnp.exp(end), 0.0))
        gains.append(gains[-1] * through[-1])
    return through, gains


def as_rows(values):
    row16 = lax.broadcasted_iota(I32, (16, LANES), 0)
    block = jnp.zeros((16, LANES), F32)
    for i, v in enumerate(values):
        block = jnp.where(row16 == i, v, block)
    return block


def stage_p(
    idx_ref, len_ref, dt_ref, al_ref, db_ref, cum_ref, step_ref, fl_ref, wst_ref, pass_ref
):
    lane = lax.broadcasted_iota(I32, (STRETCH, LANES), 1)
    row = lax.broadcasted_iota(I32, (STRETCH, LANES), 0)
    lane_f = lane.astype(F32)
    start = (-idx_ref[0] * TOK).astype(F32)
    lengths = jnp.concatenate([len_ref[...].astype(F32)] * 4, axis=1)
    earlier = jnp.where((row < lane) & (row < REQS), 1.0, 0.0)
    first = start + jnp.dot(
        jnp.broadcast_to(lengths, (8, LANES)),
        earlier,
        precision=lax.Precision.HIGHEST,
        preferred_element_type=F32,
    )[0:1, :]
    first = jnp.where(lane_f[0:1, :] < REQS, first, start)
    coef = -jnp.exp(jnp.concatenate([al_ref[...]] * 4, axis=1))
    bias = jnp.concatenate([db_ref[...]] * 4, axis=1)
    lower = jnp.where(row >= lane, 1.0, 0.0)
    through = []
    gains = [jnp.ones((1, LANES), F32)]
    for c in range(NC):
        rows = slice(c * STRETCH, (c + 1) * STRETCH)
        here = row + c * STRETCH
        started = jnp.where(first <= here.astype(F32), first, start)
        fl = jnp.broadcast_to(jnp.max(started, axis=1, keepdims=True), (STRETCH, LANES))
        fl = fl.astype(I32)
        fl_ref[rows, :] = fl
        raw = jnp.concatenate([dt_ref[:, rows]] * 4, axis=0).T + bias
        step = jnp.maximum(raw, 0.0) + jnp.log1p(jnp.exp(-jnp.abs(raw)))
        step_ref[rows, :] = step
        cum = jnp.dot(
            lower, coef * step, precision=lax.Precision.HIGHEST, preferred_element_type=F32
        )
        cum_ref[rows, :] = cum
        end, fa = cum[STRETCH - 1 :, :], fl[STRETCH - 1 :, :]
        w = jnp.exp(end - cum) * step
        wst_ref[rows, :] = split3(jnp.where(here >= fa, w, 0.0), lane)
        through.append(jnp.where(fa < c * STRETCH, jnp.exp(end), 0.0))
        gains.append(gains[-1] * through[-1])
    lane16 = lax.broadcasted_iota(I32, (16, LANES), 1)
    wst_ref[NC * STRETCH :, :] = split3(as_rows(through + gains), lane16)
    pass_ref[...] = jnp.broadcast_to(gains[NC], (16, LANES))


def stage_a(
    x_ref, xh_ref, bc_ref, bch_ref, wx_ref, bx_ref, wbc_ref, bbc_ref, fl_ref, wst_ref,
    xc_ref, bcc_ref, ent_ref, s_ref, entry_ref,
    mask_scr, spread_scr, bt_scr,
):
    s = pl.program_id(0)
    row = lax.broadcasted_iota(I32, (STRETCH, LANES), 0)

    @pl.when(s == 0)
    def _():
        for c in range(NC):
            rows = slice(c * STRETCH, (c + 1) * STRETCH)
            since = row + c * STRETCH - fl_ref[rows, :]
            for d in range(1, KW):
                mask_scr[d - 1, rows, :] = jnp.where(since >= d, 1.0, 0.0)
        for part in range(2):
            for g in range(GROUPS):
                at = slice((part * GROUPS + g) * LANES, (part * GROUPS + g + 1) * LANES)
                own = slice(g * LANES, (g + 1) * LANES)
                taps = [wbc_ref[k, part : part + 1, own] for k in range(KW)]
                off = bbc_ref[part : part + 1, own]
                for c in range(NC):
                    if c == 0:
                        ext = jnp.concatenate([bch_ref[:, at], bc_ref[0:STRETCH, at]], axis=0)
                    else:
                        ext = bc_ref[c * STRETCH - HALO : (c + 1) * STRETCH, at]
                    rows = slice(c * STRETCH, (c + 1) * STRETCH)
                    masks = [mask_scr[d, rows, :] for d in range(KW - 1)]
                    out = conv_tile(ext.astype(F32), taps, off, masks).astype(BF)
                    bcc_ref[rows, at] = out
                    if part == 0:
                        bt_scr[g * NC + c] = out.astype(F32).T.astype(BF)

    spread_scr[...] = jnp.dot(
        wst_ref[...], spread_matrix(s * (SW // HEAD_DIM), SW), preferred_element_type=F32
    )
    ex = NC * STRETCH
    group = s // (STEPS // GROUPS)
    entry_ref[...] = spread_scr[ex:, :]
    entering = None
    for c in range(NC):
        rows = slice(c * STRETCH, (c + 1) * STRETCH)
        masks = [mask_scr[d, rows, :] for d in range(KW - 1)]
        scaled = []
        for t in range(SLT):
            at = slice(t * LANES, (t + 1) * LANES)
            if c == 0:
                ext = jnp.concatenate([xh_ref[:, at], x_ref[0:STRETCH, at]], axis=0)
            else:
                ext = x_ref[c * STRETCH - HALO : (c + 1) * STRETCH, at]
            taps = [wx_ref[k : k + 1, at] for k in range(KW)]
            out = conv_tile(ext.astype(F32), taps, bx_ref[:, at], masks).astype(BF)
            xc_ref[rows, at] = out
            scaled.append((out.astype(F32) * spread_scr[rows, at]).astype(BF))
        local = jnp.dot(
            bt_scr[group * NC + c], jnp.concatenate(scaled, axis=1), preferred_element_type=F32
        )
        if c == 0:
            ent_ref[0] = jnp.zeros((STATE, SW), BF)
            entering = local
        else:
            ent_ref[c] = entering.astype(BF)
            entering = spread_scr[ex + c : ex + c + 1, :] * entering + local
    s_ref[...] = entering.astype(BF)


def stage_e(
    idx_ref, len_ref, x_ref, xh_ref, bc_ref, bch_ref, xc_ref, bcc_ref, cum_ref, step_ref, ent_ref,
    s_ref,
    piece_ref, gain_ref,
    wst_scr, spread_scr, sc_scr,
):
    s = pl.program_id(0)
    lane = lax.broadcasted_iota(I32, (STRETCH, LANES), 1)
    row = lax.broadcasted_iota(I32, (STRETCH, LANES), 0)
    ex = 2 * STRETCH

    @pl.when(s == 0)
    def _():
        count, behind, e0, f0, e1, f1, fa = scan_lengths(idx_ref, len_ref)
        sc_scr[0], sc_scr[1], sc_scr[2], sc_scr[3], sc_scr[4] = e0, f0, e1, f1, count
        inflow = []
        for k, (e, f) in enumerate(((e0, f0), (e1, f1))):
            base = pl.multiple_of((e >> 7) * STRETCH, STRETCH)
            here = row + base
            end = cum_ref[pl.ds(e, 1), :]
            w = jnp.exp(end - cum_ref[pl.ds(base, STRETCH), :]) * step_ref[pl.ds(base, STRETCH), :]
            w = jnp.where((here >= f) & (here <= e), w, 0.0)
            wst_scr[k * STRETCH : (k + 1) * STRETCH, :] = split3(w, lane)
            inflow.append(jnp.where(f < base, jnp.exp(end), 0.0))
        _, gains = stretch_gains(cum_ref, fa)
        gain = gains[0]
        for c in range(1, NC):
            gain = jnp.where((e0 >> 7) == c, gains[c], gain)
        gain = gain * inflow[0]
        by_owner = jnp.where((count > 0) & (behind == 0), gain, 0.0)
        by_sender = jnp.where(count == 0, gains[NC], jnp.where(behind == 0, 0.0, gain))
        lane16 = lax.broadcasted_iota(I32, (16, LANES), 1)
        wst_scr[ex:, :] = split3(as_rows(inflow + [by_owner, by_sender]), lane16)

    e0, f0, e1, f1 = sc_scr[0], sc_scr[1], sc_scr[2], sc_scr[3]
    spread_scr[...] = jnp.dot(
        wst_scr[...], spread_matrix(s * (SW // HEAD_DIM), SW), preferred_element_type=F32
    )
    gain_ref[...] = jnp.broadcast_to(spread_scr[ex + 3 : ex + 4, :], (8, SW))
    group = s // (STEPS // GROUPS)
    for k, e in enumerate((e0, e1)):
        c = e >> 7
        base = pl.multiple_of(c * STRETCH, STRETCH)
        at = k * STRETCH
        scaled = (
            xc_ref[pl.ds(base, STRETCH), :].astype(F32) * spread_scr[at : at + STRETCH, :]
        ).astype(BF)
        b = jnp.where(
            group == 0,
            bcc_ref[pl.ds(base, STRETCH), 0:LANES].astype(F32),
            bcc_ref[pl.ds(base, STRETCH), LANES : 2 * LANES].astype(F32),
        )
        final = spread_scr[ex + k : ex + k + 1, :] * ent_ref[c].astype(F32) + jnp.dot(
            b.T.astype(BF), scaled, preferred_element_type=F32
        )
        if k == 0:
            final = jnp.where(sc_scr[4] == 0, s_ref[...].astype(F32), final)
        final = final.astype(BF)
        for j in range(2 * SLT):
            piece_ref[j, k * 64 : k * 64 + 64, :] = final[
                (j % 2) * 64 : (j % 2) * 64 + 64, (j // 2) * LANES : (j // 2 + 1) * LANES
            ]

    tails_x, tails_bc = [], []
    pick_row = lax.broadcasted_iota(I32, (16, 2 * HALO), 0)
    pick_col = lax.broadcasted_iota(I32, (16, 2 * HALO), 1)
    for e, f in ((e0, f0), (e1, f1)):
        base = pl.multiple_of((e >> 4) * HALO, HALO)
        before = pl.multiple_of(jnp.maximum(base - HALO, 0), HALO)
        source = e - (KW - 2) + pick_row
        pick = (pick_col + base - HALO == source) & (source >= f) & (pick_row < KW - 1)
        pick = jnp.where(pick, 1.0, 0.0).astype(BF)

        def tail(ref, halo_ref):
            head = jnp.where(base > 0, ref[pl.ds(before, HALO), :], halo_ref[...])
            window = jnp.concatenate([head, ref[pl.ds(base, HALO), :]], axis=0)
            return jnp.dot(pick, window, preferred_element_type=F32)

        tails_x.append(tail(x_ref, xh_ref))
        tails_bc.append(tail(bc_ref, bch_ref))
    row16 = lax.broadcasted_iota(I32, (16, LANES), 0)
    for t in range(SLT):
        at = slice(t * LANES, (t + 1) * LANES)
        gain = spread_scr[ex + 2 : ex + 3, at]
        gain_hi = gain.astype(BF).astype(F32)
        bc_rows = []
        for k in range(2):
            one = tails_bc[k][:, at]
            bc_rows.append(jnp.sum(jnp.where(row16 == s, one, 0.0), axis=0, keepdims=True))
        for half in range(2):
            values = [gain_hi, gain - gain_hi]
            for k in range(2):
                one = tails_x[k][:, at]
                values += [one[0:1], one[1:2]] if half == 0 else [one[2:3], bc_rows[k]]
            piece_ref[2 * t + half, 128:136, :] = as_rows(values)[0:8].astype(BF)


def stage_b(xc_ref, bcc_ref, cum_ref, step_ref, fl_ref, skip_ref, y_ref):
    c = pl.program_id(0)
    row = lax.broadcasted_iota(I32, (STRETCH, LANES), 0)
    lane = lax.broadcasted_iota(I32, (STRETCH, LANES), 1)
    keep = (lane <= row) & (lane + c * STRETCH >= fl_ref[...])
    cum = cum_ref[...]
    cum_t = cum.T
    step_t = step_ref[...].T
    low = lax.broadcasted_iota(I32, (STRETCH, LANES), 1) < HEAD_DIM
    for g in range(GROUPS):
        b = bcc_ref[:, g * LANES : (g + 1) * LANES]
        cc = bcc_ref[:, (GROUPS + g) * LANES : (GROUPS + g + 1) * LANES]
        scores = lax.dot_general(cc, b, (((1,), (1,)), ((), ())), preferred_element_type=F32)
        for i in range(HEADS // GROUPS // 2):
            pair = g * (HEADS // GROUPS // 2) + i
            weights = []
            for h in (2 * pair, 2 * pair + 1):
                decay = jnp.exp(jnp.where(keep, cum[:, h : h + 1] - cum_t[h : h + 1, :], -jnp.inf))
                weights.append((scores * (decay * step_t[h : h + 1, :])).astype(BF))
            at = slice(pair * LANES, (pair + 1) * LANES)
            x = xc_ref[:, at]
            xf = x.astype(F32)
            both = jnp.concatenate(
                [jnp.where(low, xf, 0.0).astype(BF), jnp.where(low, 0.0, xf).astype(BF)], axis=0
            )
            inner = jnp.dot(
                jnp.concatenate(weights, axis=1), both, preferred_element_type=F32
            )
            y_ref[:, at] = inner + skip_ref[:, at] * xf


def stage_c(
    y_ref, z_ref, c_ref, ent_ref, s1_ref, s2_ref, far_ref, far_gain_ref, entry_ref, cum_ref, fl_ref, gain_ref, out_ref
):
    g, c = pl.program_id(0), pl.program_id(1)
    lane = lax.broadcasted_iota(I32, (STRETCH, LANES), 1)
    inflow = jnp.where(fl_ref[...] < c * STRETCH, jnp.exp(cum_ref[...]), 0.0)
    both = jnp.concatenate([split3(inflow, lane), split3(far_gain_ref[...], lane[0:16])], axis=0)
    wide = jnp.dot(
        both, spread_matrix(g * (HEADS // GROUPS), GWIDTH), preferred_element_type=F32
    )
    far_gain = wide[STRETCH : STRETCH + 1, :]
    wide = wide[0:STRETCH, :]
    incoming = s1_ref[...].astype(F32) + s2_ref[...].astype(F32)
    incoming = incoming + far_gain * far_ref[...].astype(F32)
    entering = ent_ref[0].astype(F32) + entry_ref[pl.ds(NC + c, 1), :] * incoming
    carried = jnp.dot(c_ref[...], entering.astype(BF), preferred_element_type=F32)
    gated = (y_ref[...] + wide * carried) * swish(z_ref[...].astype(F32))
    mean = jnp.sum(gated * gated, axis=1, keepdims=True) * (1.0 / GWIDTH)
    out_ref[...] = (gated * lax.rsqrt(mean + EPS) * gain_ref[...]).astype(BF)


def add_incoming(piece_ref, s1_ref, gain_ref, out_ref):
    for j in range(out_ref.shape[0]):
        at = slice((j // 2) * LANES, (j // 2 + 1) * LANES)
        came = s1_ref[(j % 2) * 64 : (j % 2) * 64 + 64, at].astype(F32)
        out_ref[j] = (piece_ref[j].astype(F32) + gain_ref[0:1, at] * came).astype(BF)


def pass_on(s1_ref, entry_ref, out_ref):
    out_ref[...] = (entry_ref[8:9, :] * s1_ref[...].astype(F32)).astype(BF)


def combine(len_ref, owner_ref, got_ref, out_ref):
    row8 = lax.broadcasted_iota(I32, (8, LANES), 0)

    def one(r, carry):
        first, before = carry
        last = first + len_ref[0, r] - 1
        home = last >> 9
        second = before == home
        h1 = jnp.maximum(home - 1, 0)
        slot = owner_ref[0, r]
        extra = got_ref[home, 128:136, :].astype(F32)
        gain = jnp.where(second, 0.0, extra[0:1] + extra[1:2])
        k = pl.multiple_of(jnp.where(second, 64, 0), 64)
        own = got_ref[home, pl.ds(k, 64), :].astype(F32)
        out_ref[slot, 0:64, :] = (own + gain * got_ref[h1, 0:64, :].astype(F32)).astype(BF)
        tail = jnp.where(second, pltpu.roll(extra, 4, 0), pltpu.roll(extra, 6, 0))
        out_ref[slot, 64:72, :] = jnp.where(row8 < 2, tail, 0.0).astype(BF)
        return last + 1, home

    lax.fori_loop(0, REQS, one, (jnp.int32(0), jnp.int32(-1)), unroll=2)


def finish(got_ref, state_ref, tx_ref, tbc_ref):
    tails = [got_ref[j, 64:72, :].astype(F32) for j in range(REQS)]
    for t in range(WIDTH // LANES):
        at = slice(t * LANES, (t + 1) * LANES)
        block = jnp.concatenate(
            [got_ref[2 * t, 0:64, :], got_ref[2 * t + 1, 0:64, :]], axis=0
        ).astype(F32)
        turned = block.T
        state_ref[2 * t] = turned[0:64]
        state_ref[2 * t + 1] = turned[64:128]
        tx_ref[:, at] = jnp.concatenate([tails[2 * t][0:2], tails[2 * t + 1][0:1]], axis=0).astype(BF)
    for k in range(KW - 1):
        for q in range(4):
            value = tails[2 * (4 * k + q) + 1][1:2].astype(BF)
            tbc_ref[k, q // 2 : q // 2 + 1, (q % 2) * LANES : (q % 2 + 1) * LANES] = value


def call(kernel, grid, ins, outs, scratch=(), flops=0, nbytes=0, aliases=None, limit=None):
    return pl.pallas_call(
        kernel,
        grid=grid,
        in_specs=ins,
        out_specs=[o[1] for o in outs],
        out_shape=[o[0] for o in outs],
        scratch_shapes=list(scratch),
        input_output_aliases=aliases or {},
        compiler_params=pltpu.CompilerParams(vmem_limit_bytes=limit or LARGE),
        cost_estimate=pl.CostEstimate(flops=flops, bytes_accessed=nbytes, transcendentals=0),
    )


def whole(*shape):
    return pl.BlockSpec(shape, lambda *_: (0,) * len(shape))


def on_device(
    x_in, bc_in, z_in, dt_in, conv_x_w, conv_x_b, conv_bc_w, conv_bc_b, a_log, dt_bias, skip_d,
    norm_gain, lengths, owner_slot,
):
    x = x_in[0]
    bc = bc_in[0].reshape(TOK, BCW)
    z = z_in[0]
    index = lax.axis_index("ctx").astype(I32).reshape(1)
    smem = pl.BlockSpec(memory_space=pltpu.SMEM)
    shape = jax.ShapeDtypeStruct
    cols = lambda rows: pl.BlockSpec((rows, SW), lambda s: (0, s))
    ends = bc_in[0, TOK - HALO :].reshape(HALO, BCW)
    halo = shift_in(jnp.concatenate([x[TOK - HALO :], ends], axis=1), 1)
    halo_cols = pl.BlockSpec((HALO, BCW), lambda s: (0, WIDTH // BCW))

    vmem = pl.BlockSpec(memory_space=pltpu.VMEM)
    by_head = shape((TOK, LANES), F32)
    cum, step, fl, wst, passing = call(
        stage_p,
        (),
        [smem, vmem, vmem, vmem, vmem],
        [
            (by_head, vmem),
            (by_head, vmem),
            (shape((TOK, LANES), I32), vmem),
            (shape((TOK + 16, LANES), BF), vmem),
            (shape((16, LANES), F32), vmem),
        ],
        flops=10**8,
        nbytes=2**20,
    )(index, lengths, dt_in[0].T, a_log.reshape(1, HEADS), dt_bias.reshape(1, HEADS))

    xc, bcc, ent, left, entry = call(
        stage_a,
        (STEPS,),
        [
            cols(TOK),
            cols(HALO),
            whole(TOK, BCW),
            halo_cols,
            cols(KW),
            cols(1),
            whole(KW, 2, 2 * LANES),
            whole(2, 2 * LANES),
            whole(TOK, LANES),
            whole(TOK + 16, LANES),
        ],
        [
            (shape((TOK, WIDTH), BF), cols(TOK)),
            (shape((TOK, BCW), BF), whole(TOK, BCW)),
            (
                shape((NC, STATE, WIDTH), BF),
                pl.BlockSpec((NC, STATE, SW), lambda s: (0, 0, s)),
            ),
            (shape((STATE, WIDTH), BF), cols(STATE)),
            (shape((16, WIDTH), F32), cols(16)),
        ],
        [
            pltpu.VMEM((KW - 1, TOK, LANES), F32),
            pltpu.VMEM((TOK + 16, SW), F32),
            pltpu.VMEM((GROUPS * NC, STATE, STRETCH), BF),
        ],
        flops=10**9,
        nbytes=10 * 2**20,
    )(
        x, halo, bc, halo, conv_x_w, conv_x_b.reshape(1, WIDTH), conv_bc_w, conv_bc_b, fl, wst
    )

    s1 = shift_in(left, 1)
    crossed = shift_pairs(left, ROW_Y - 1, (ROW_Y - 2,))
    far_gain = shift_pairs(passing, 1, (ROW_Y - 1,))

    pieces, gain = call(
        stage_e,
        (STEPS,),
        [
            smem,
            smem,
            cols(TOK),
            cols(HALO),
            whole(TOK, BCW),
            halo_cols,
            cols(TOK),
            whole(TOK, BCW),
            whole(TOK, LANES),
            whole(TOK, LANES),
            pl.BlockSpec((NC, STATE, SW), lambda s: (0, 0, s)),
            cols(STATE),
        ],
        [
            (
                shape((32, PIECE, LANES), BF),
                pl.BlockSpec((2 * SLT, PIECE, LANES), lambda s: (s, 0, 0)),
            ),
            (shape((8, WIDTH), F32), cols(8)),
        ],
        [
            pltpu.VMEM((2 * STRETCH + 16, LANES), BF),
            pltpu.VMEM((2 * STRETCH + 16, SW), F32),
            pltpu.SMEM((5,), I32),
        ],
        flops=5 * 10**8,
        nbytes=8 * 2**20,
    )(index, lengths, x, halo, bc, halo, xc, bcc, cum, step, ent, left)

    by_row = lambda width: pl.BlockSpec((STRETCH, width), lambda c: (c, 0))
    (y,) = call(
        stage_b,
        (NC,),
        [by_row(WIDTH), by_row(BCW), by_row(LANES), by_row(LANES), by_row(LANES), whole(1, WIDTH)],
        [(shape((TOK, WIDTH), F32), by_row(WIDTH))],
        flops=10**9,
        nbytes=20 * 2**20,
    )(xc, bcc, cum, step, fl, jnp.repeat(skip_d, HEAD_DIM).reshape(1, WIDTH))

    s1, crossed = lax.optimization_barrier((s1, crossed))
    part = pl.BlockSpec((16, 64, LANES), lambda s: (s, 0, 0))
    half = lambda rows: pl.BlockSpec((rows, GWIDTH), lambda s: (0, s))
    (pieces,) = call(
        add_incoming,
        (2,),
        [part, half(STATE), half(8)],
        [(shape((32, PIECE, LANES), BF), part)],
        flops=10**7,
        nbytes=2 * 2**20,
        aliases={0: 0},
    )(pieces, s1, gain)
    got = lax.all_to_all(pieces, "ctx", split_axis=0, concat_axis=0, tiled=True)

    (passed,) = call(
        pass_on,
        (2,),
        [half(STATE), half(16)],
        [(shape((STATE, WIDTH), BF), half(STATE))],
        flops=10**7,
        nbytes=2 * 2**20,
        limit=SMALL,
    )(s1, entry)
    s2 = shift_pairs(passed, 1, range(ROW_Y - 1))
    count = lax.axis_size("ctx")
    far = lax.ppermute(crossed, "ctx", [(i + 1, i) for i in range(0, count, ROW_Y)])

    got, s2, far, far_gain, y = lax.optimization_barrier((got, s2, far, far_gain, y))
    (back,) = call(
        combine,
        (),
        [smem, smem, pl.BlockSpec(memory_space=pltpu.VMEM)],
        [(shape((REQS, BACK, LANES), BF), pl.BlockSpec(memory_space=pltpu.VMEM))],
        flops=10**7,
        nbytes=3 * 2**20,
        limit=SMALL,
    )(lengths, owner_slot, got)
    own = lax.all_to_all(back, "ctx", split_axis=0, concat_axis=0, tiled=True)

    back, y = lax.optimization_barrier((back, y))
    by_c = lambda g, c: (c, 0)
    by_g = lambda g, c: (0, g)
    by_cg = lambda g, c: (c, g)
    (mixed,) = call(
        stage_c,
        (GROUPS, NC),
        [
            pl.BlockSpec((STRETCH, GWIDTH), by_cg),
            pl.BlockSpec((STRETCH, GWIDTH), by_cg),
            pl.BlockSpec((STRETCH, LANES), lambda g, c: (c, GROUPS + g)),
            pl.BlockSpec((1, STATE, GWIDTH), lambda g, c: (c, 0, g)),
            pl.BlockSpec((STATE, GWIDTH), by_g),
            pl.BlockSpec((STATE, GWIDTH), by_g),
            pl.BlockSpec((STATE, GWIDTH), by_g),
            whole(16, LANES),
            pl.BlockSpec((16, GWIDTH), by_g),
            pl.BlockSpec((STRETCH, LANES), by_c),
            pl.BlockSpec((STRETCH, LANES), by_c),
            pl.BlockSpec((1, GWIDTH), by_g),
        ],
        [(shape((TOK, WIDTH), BF), pl.BlockSpec((STRETCH, GWIDTH), by_cg))],
        flops=10**9,
        nbytes=15 * 2**20,
    )(y, z, bcc, ent, s1, s2, far, far_gain, entry, cum, fl, norm_gain.reshape(1, WIDTH))

    own, mixed = lax.optimization_barrier((own, mixed))
    swapped = lax.ppermute(own, "side", [(0, 1), (1, 0)])
    state, tail_x, tail_bc = call(
        finish,
        (),
        [pl.BlockSpec(memory_space=pltpu.VMEM)],
        [
            (shape((HEADS, HEAD_DIM, STATE), F32), pl.BlockSpec(memory_space=pltpu.VMEM)),
            (shape((KW - 1, WIDTH), BF), pl.BlockSpec(memory_space=pltpu.VMEM)),
            (shape((KW - 1, 2, 2 * LANES), BF), pl.BlockSpec(memory_space=pltpu.VMEM)),
        ],
        flops=10**7,
        nbytes=3 * 2**20,
        limit=SMALL,
    )(swapped)
    return mixed[None], state[None, None], tail_x[None, None], tail_bc[None, None]


def solution(mesh):
    placed = (
        P("side", "ctx", "head"),
        P("side", "ctx", None, "head"),
        P("side", "ctx", "head"),
        P("side", "ctx", "head"),
        P(None, "head"),
        P("head"),
        P(None, None, "head"),
        P(None, "head"),
        P("head"),
        P("head"),
        P("head"),
        P("head"),
        P("side", None),
        P("side", None),
    )
    return jax.shard_map(
        on_device,
        mesh=mesh,
        in_specs=placed,
        out_specs=(
            P("side", "ctx", "head"),
            P("side", "ctx", "head", None, None),
            P("side", "ctx", None, "head"),
            P("side", "ctx", None, None, "head"),
        ),
        check_vma=False,
    )
```

```python
import jax
import jax.numpy as jnp
from jax import lax
from jax.experimental import pallas as pl
from jax.experimental.pallas import tpu as pltpu
from jax.sharding import PartitionSpec as P

HEAD_DIM = 64
STATE = 128
STRETCH = 128
LANES = 128
HALO = 16
KW = 4
EPS = 1e-05
BF = jnp.bfloat16
F32 = jnp.float32
I32 = jnp.int32
LARGE = 60 * 1024 * 1024
SMALL = 16 * 1024 * 1024

TOK = 512
NC = TOK // STRETCH
WIDTH = 2048
HEADS = WIDTH // HEAD_DIM
GROUPS = 2
GWIDTH = WIDTH // GROUPS
BCW = 512
REQS = 32
ROW_Y = 4
STEPS = 4
SW = WIDTH // STEPS
SLT = SW // LANES
PIECE = 2 * 64 + 16
BACK = 64 + 16


def shift_in(block, distance):
    count = lax.axis_size("ctx")
    return lax.ppermute(block, "ctx", [(i, i + distance) for i in range(count - distance)])


def shift_pairs(block, distance, keep):
    count = lax.axis_size("ctx")
    pairs = [(i, i + distance) for i in range(count - distance) if i % ROW_Y in keep]
    return lax.ppermute(block, "ctx", pairs)


def swish(v):
    half = 0.5 * v
    return half + half * jnp.tanh(half)


def split3(v, lane):
    hi = v.astype(BF).astype(F32)
    rest = v - hi
    mid = rest.astype(BF).astype(F32)
    low = rest - mid
    return jnp.where(
        lane < HEADS, hi, jnp.where(lane < 2 * HEADS, mid, jnp.where(lane < 3 * HEADS, low, 0.0))
    ).astype(BF)


def spread_matrix(first_head, width):
    row = lax.broadcasted_iota(I32, (LANES, width), 0)
    col = lax.broadcasted_iota(I32, (LANES, width), 1)
    same = ((row & (HEADS - 1)) == (col >> 6) + first_head) & (row < 3 * HEADS)
    return jnp.where(same, 1.0, 0.0).astype(BF)


def conv_tile(ext, taps, bias, masks):
    half = 0.5 * bias + (0.5 * taps[KW - 1]) * ext[HALO:]
    for d in range(1, KW):
        half = half + (0.5 * taps[KW - 1 - d]) * (pltpu.roll(ext, d, 0)[HALO:] * masks[d - 1])
    return half + half * jnp.tanh(half)


def scan_lengths(idx_ref, len_ref):
    zero = jnp.int32(0)

    def scan(r, carry):
        first, count, behind, e0, f0, e1, f1, fa = carry
        last = first + len_ref[0, r] - 1
        ends = (last >= 0) & (last < TOK)
        take0, take1 = ends & (count == 0), ends & (count == 1)
        points = [c * STRETCH + STRETCH - 1 for c in range(NC)]
        fa = tuple(
            jnp.where((first <= p) & (last >= p), first, old) for p, old in zip(points, fa)
        )
        return (
            last + 1,
            count + jnp.where(ends, 1, 0),
            behind + jnp.where((last >= -TOK) & (last < 0), 1, 0),
            jnp.where(take0, last, e0),
            jnp.where(take0, first, f0),
            jnp.where(take1, last, e1),
            jnp.where(take1, first, f1),
            fa,
        )

    start = -idx_ref[0] * TOK
    out = lax.fori_loop(
        0, REQS, scan, (start, zero, zero, zero, zero, zero, zero, (zero,) * NC), unroll=4
    )
    return out[1:]


def stretch_gains(cum_ref, fa):
    through = []
    gains = [jnp.ones((1, LANES), F32)]
    for c in range(NC):
        end = cum_ref[(c + 1) * STRETCH - 1 : (c + 1) * STRETCH, :]
        through.append(jnp.where(fa[c] < c * STRETCH, jnp.exp(end), 0.0))
        gains.append(gains[-1] * through[-1])
    return through, gains


def as_rows(values):
    row16 = lax.broadcasted_iota(I32, (16, LANES), 0)
    block = jnp.zeros((16, LANES), F32)
    for i, v in enumerate(values):
        block = jnp.where(row16 == i, v, block)
    return block


def stage_p(
    idx_ref, len_ref, dt_ref, al_ref, db_ref, cum_ref, step_ref, fl_ref, wst_ref, pass_ref
):
    lane = lax.broadcasted_iota(I32, (STRETCH, LANES), 1)
    row = lax.broadcasted_iota(I32, (STRETCH, LANES), 0)
    lane_f = lane.astype(F32)
    start = (-idx_ref[0] * TOK).astype(F32)
    lengths = jnp.concatenate([len_ref[...].astype(F32)] * 4, axis=1)
    earlier = jnp.where((row < lane) & (row < REQS), 1.0, 0.0)
    first = start + jnp.dot(
        jnp.broadcast_to(lengths, (8, LANES)),
        earlier,
        precision=lax.Precision.HIGHEST,
        preferred_element_type=F32,
    )[0:1, :]
    first = jnp.where(lane_f[0:1, :] < REQS, first, start)
    coef = -jnp.exp(jnp.concatenate([al_ref[...]] * 4, axis=1))
    bias = jnp.concatenate([db_ref[...]] * 4, axis=1)
    lower = jnp.where(row >= lane, 1.0, 0.0)
    through = []
    gains = [jnp.ones((1, LANES), F32)]
    for c in range(NC):
        rows = slice(c * STRETCH, (c + 1) * STRETCH)
        here = row + c * STRETCH
        started = jnp.where(first <= here.astype(F32), first, start)
        fl = jnp.broadcast_to(jnp.max(started, axis=1, keepdims=True), (STRETCH, LANES))
        fl = fl.astype(I32)
        fl_ref[rows, :] = fl
        raw = jnp.concatenate([dt_ref[:, rows]] * 4, axis=0).T + bias
        step = jnp.maximum(raw, 0.0) + jnp.log1p(jnp.exp(-jnp.abs(raw)))
        step_ref[rows, :] = step
        cum = jnp.dot(
            lower, coef * step, precision=lax.Precision.HIGHEST, preferred_element_type=F32
        )
        cum_ref[rows, :] = cum
        end, fa = cum[STRETCH - 1 :, :], fl[STRETCH - 1 :, :]
        w = jnp.exp(end - cum) * step
        wst_ref[rows, :] = split3(jnp.where(here >= fa, w, 0.0), lane)
        through.append(jnp.where(fa < c * STRETCH, jnp.exp(end), 0.0))
        gains.append(gains[-1] * through[-1])
    lane16 = lax.broadcasted_iota(I32, (16, LANES), 1)
    wst_ref[NC * STRETCH :, :] = split3(as_rows(through + gains), lane16)
    pass_ref[...] = jnp.broadcast_to(gains[NC], (16, LANES))


def stage_a(
    x_ref, xh_ref, bc_ref, bch_ref, wx_ref, bx_ref, wbc_ref, bbc_ref, fl_ref, wst_ref,
    xc_ref, bcc_ref, ent_ref, s_ref, entry_ref,
    mask_scr, spread_scr, bt_scr,
):
    s = pl.program_id(0)
    row = lax.broadcasted_iota(I32, (STRETCH, LANES), 0)

    @pl.when(s == 0)
    def _():
        for c in range(NC):
            rows = slice(c * STRETCH, (c + 1) * STRETCH)
            since = row + c * STRETCH - fl_ref[rows, :]
            for d in range(1, KW):
                mask_scr[d - 1, rows, :] = jnp.where(since >= d, 1.0, 0.0)
        for part in range(2):
            for g in range(GROUPS):
                at = slice((part * GROUPS + g) * LANES, (part * GROUPS + g + 1) * LANES)
                own = slice(g * LANES, (g + 1) * LANES)
                taps = [wbc_ref[k, part : part + 1, own] for k in range(KW)]
                off = bbc_ref[part : part + 1, own]
                for c in range(NC):
                    if c == 0:
                        ext = jnp.concatenate([bch_ref[:, at], bc_ref[0:STRETCH, at]], axis=0)
                    else:
                        ext = bc_ref[c * STRETCH - HALO : (c + 1) * STRETCH, at]
                    rows = slice(c * STRETCH, (c + 1) * STRETCH)
                    masks = [mask_scr[d, rows, :] for d in range(KW - 1)]
                    out = conv_tile(ext.astype(F32), taps, off, masks).astype(BF)
                    bcc_ref[rows, at] = out
                    if part == 0:
                        bt_scr[g * NC + c] = out.astype(F32).T.astype(BF)

    spread_scr[...] = jnp.dot(
        wst_ref[...], spread_matrix(s * (SW // HEAD_DIM), SW), preferred_element_type=F32
    )
    ex = NC * STRETCH
    group = s // (STEPS // GROUPS)
    entry_ref[...] = spread_scr[ex:, :]
    entering = None
    for c in range(NC):
        rows = slice(c * STRETCH, (c + 1) * STRETCH)
        masks = [mask_scr[d, rows, :] for d in range(KW - 1)]
        scaled = []
        for t in range(SLT):
            at = slice(t * LANES, (t + 1) * LANES)
            if c == 0:
                ext = jnp.concatenate([xh_ref[:, at], x_ref[0:STRETCH, at]], axis=0)
            else:
                ext = x_ref[c * STRETCH - HALO : (c + 1) * STRETCH, at]
            taps = [wx_ref[k : k + 1, at] for k in range(KW)]
            out = conv_tile(ext.astype(F32), taps, bx_ref[:, at], masks).astype(BF)
            xc_ref[rows, at] = out
            scaled.append((out.astype(F32) * spread_scr[rows, at]).astype(BF))
        local = jnp.dot(
            bt_scr[group * NC + c], jnp.concatenate(scaled, axis=1), preferred_element_type=F32
        )
        if c == 0:
            ent_ref[0] = jnp.zeros((STATE, SW), BF)
            entering = local
        else:
            ent_ref[c] = entering.astype(BF)
            entering = spread_scr[ex + c : ex + c + 1, :] * entering + local
    s_ref[...] = entering.astype(BF)


def stage_e(
    idx_ref, len_ref, x_ref, xh_ref, bc_ref, bch_ref, xc_ref, bcc_ref, cum_ref, step_ref, ent_ref,
    s_ref,
    piece_ref, gain_ref,
    wst_scr, spread_scr, sc_scr,
):
    s = pl.program_id(0)
    lane = lax.broadcasted_iota(I32, (STRETCH, LANES), 1)
    row = lax.broadcasted_iota(I32, (STRETCH, LANES), 0)
    ex = 2 * STRETCH

    @pl.when(s == 0)
    def _():
        count, behind, e0, f0, e1, f1, fa = scan_lengths(idx_ref, len_ref)
        sc_scr[0], sc_scr[1], sc_scr[2], sc_scr[3], sc_scr[4] = e0, f0, e1, f1, count
        inflow = []
        for k, (e, f) in enumerate(((e0, f0), (e1, f1))):
            base = pl.multiple_of((e >> 7) * STRETCH, STRETCH)
            here = row + base
            end = cum_ref[pl.ds(e, 1), :]
            w = jnp.exp(end - cum_ref[pl.ds(base, STRETCH), :]) * step_ref[pl.ds(base, STRETCH), :]
            w = jnp.where((here >= f) & (here <= e), w, 0.0)
            wst_scr[k * STRETCH : (k + 1) * STRETCH, :] = split3(w, lane)
            inflow.append(jnp.where(f < base, jnp.exp(end), 0.0))
        _, gains = stretch_gains(cum_ref, fa)
        gain = gains[0]
        for c in range(1, NC):
            gain = jnp.where((e0 >> 7) == c, gains[c], gain)
        gain = gain * inflow[0]
        by_owner = jnp.where((count > 0) & (behind == 0), gain, 0.0)
        by_sender = jnp.where(count == 0, gains[NC], jnp.where(behind == 0, 0.0, gain))
        lane16 = lax.broadcasted_iota(I32, (16, LANES), 1)
        wst_scr[ex:, :] = split3(as_rows(inflow + [by_owner, by_sender]), lane16)

    e0, f0, e1, f1 = sc_scr[0], sc_scr[1], sc_scr[2], sc_scr[3]
    spread_scr[...] = jnp.dot(
        wst_scr[...], spread_matrix(s * (SW // HEAD_DIM), SW), preferred_element_type=F32
    )
    gain_ref[...] = jnp.broadcast_to(spread_scr[ex + 3 : ex + 4, :], (8, SW))
    group = s // (STEPS // GROUPS)
    for k, e in enumerate((e0, e1)):
        c = e >> 7
        base = pl.multiple_of(c * STRETCH, STRETCH)
        at = k * STRETCH
        scaled = (
            xc_ref[pl.ds(base, STRETCH), :].astype(F32) * spread_scr[at : at + STRETCH, :]
        ).astype(BF)
        b = jnp.where(
            group == 0,
            bcc_ref[pl.ds(base, STRETCH), 0:LANES].astype(F32),
            bcc_ref[pl.ds(base, STRETCH), LANES : 2 * LANES].astype(F32),
        )
        final = spread_scr[ex + k : ex + k + 1, :] * ent_ref[c].astype(F32) + jnp.dot(
            b.T.astype(BF), scaled, preferred_element_type=F32
        )
        if k == 0:
            final = jnp.where(sc_scr[4] == 0, s_ref[...].astype(F32), final)
        final = final.astype(BF)
        for j in range(2 * SLT):
            piece_ref[j, k * 64 : k * 64 + 64, :] = final[
                (j % 2) * 64 : (j % 2) * 64 + 64, (j // 2) * LANES : (j // 2 + 1) * LANES
            ]

    tails_x, tails_bc = [], []
    pick_row = lax.broadcasted_iota(I32, (16, 2 * HALO), 0)
    pick_col = lax.broadcasted_iota(I32, (16, 2 * HALO), 1)
    for e, f in ((e0, f0), (e1, f1)):
        base = pl.multiple_of((e >> 4) * HALO, HALO)
        before = pl.multiple_of(jnp.maximum(base - HALO, 0), HALO)
        source = e - (KW - 2) + pick_row
        pick = (pick_col + base - HALO == source) & (source >= f) & (pick_row < KW - 1)
        pick = jnp.where(pick, 1.0, 0.0).astype(BF)

        def tail(ref, halo_ref):
            head = jnp.where(base > 0, ref[pl.ds(before, HALO), :], halo_ref[...])
            window = jnp.concatenate([head, ref[pl.ds(base, HALO), :]], axis=0)
            return jnp.dot(pick, window, preferred_element_type=F32)

        tails_x.append(tail(x_ref, xh_ref))
        tails_bc.append(tail(bc_ref, bch_ref))
    row16 = lax.broadcasted_iota(I32, (16, LANES), 0)
    for t in range(SLT):
        at = slice(t * LANES, (t + 1) * LANES)
        gain = spread_scr[ex + 2 : ex + 3, at]
        gain_hi = gain.astype(BF).astype(F32)
        bc_rows = []
        for k in range(2):
            one = tails_bc[k][:, at]
            bc_rows.append(jnp.sum(jnp.where(row16 == s, one, 0.0), axis=0, keepdims=True))
        for half in range(2):
            values = [gain_hi, gain - gain_hi]
            for k in range(2):
                one = tails_x[k][:, at]
                values += [one[0:1], one[1:2]] if half == 0 else [one[2:3], bc_rows[k]]
            piece_ref[2 * t + half, 128:144, :] = as_rows(values).astype(BF)


def stage_b(xc_ref, bcc_ref, cum_ref, step_ref, fl_ref, skip_ref, y_ref):
    c = pl.program_id(0)
    row = lax.broadcasted_iota(I32, (STRETCH, LANES), 0)
    lane = lax.broadcasted_iota(I32, (STRETCH, LANES), 1)
    keep = (lane <= row) & (lane + c * STRETCH >= fl_ref[...])
    cum = cum_ref[...]
    cum_t = cum.T
    step_t = step_ref[...].T
    low = lax.broadcasted_iota(I32, (STRETCH, LANES), 1) < HEAD_DIM
    for g in range(GROUPS):
        b = bcc_ref[:, g * LANES : (g + 1) * LANES]
        cc = bcc_ref[:, (GROUPS + g) * LANES : (GROUPS + g + 1) * LANES]
        scores = lax.dot_general(cc, b, (((1,), (1,)), ((), ())), preferred_element_type=F32)
        for i in range(HEADS // GROUPS // 2):
            pair = g * (HEADS // GROUPS // 2) + i
            weights = []
            for h in (2 * pair, 2 * pair + 1):
                decay = jnp.exp(jnp.where(keep, cum[:, h : h + 1] - cum_t[h : h + 1, :], -jnp.inf))
                weights.append((scores * (decay * step_t[h : h + 1, :])).astype(BF))
            at = slice(pair * LANES, (pair + 1) * LANES)
            x = xc_ref[:, at]
            xf = x.astype(F32)
            both = jnp.concatenate(
                [jnp.where(low, xf, 0.0).astype(BF), jnp.where(low, 0.0, xf).astype(BF)], axis=0
            )
            inner = jnp.dot(
                jnp.concatenate(weights, axis=1), both, preferred_element_type=F32
            )
            y_ref[:, at] = inner + skip_ref[:, at] * xf


def stage_c(
    y_ref, z_ref, c_ref, ent_ref, s1_ref, s2_ref, far_ref, far_gain_ref, entry_ref, cum_ref, fl_ref, gain_ref, out_ref
):
    g, c = pl.program_id(0), pl.program_id(1)
    lane = lax.broadcasted_iota(I32, (STRETCH, LANES), 1)
    inflow = jnp.where(fl_ref[...] < c * STRETCH, jnp.exp(cum_ref[...]), 0.0)
    both = jnp.concatenate([split3(inflow, lane), split3(far_gain_ref[...], lane[0:16])], axis=0)
    wide = jnp.dot(
        both, spread_matrix(g * (HEADS // GROUPS), GWIDTH), preferred_element_type=F32
    )
    far_gain = wide[STRETCH : STRETCH + 1, :]
    wide = wide[0:STRETCH, :]
    incoming = s1_ref[...].astype(F32) + s2_ref[...].astype(F32)
    incoming = incoming + far_gain * far_ref[...].astype(F32)
    entering = ent_ref[0].astype(F32) + entry_ref[pl.ds(NC + c, 1), :] * incoming
    carried = jnp.dot(c_ref[...], entering.astype(BF), preferred_element_type=F32)
    gated = (y_ref[...] + wide * carried) * swish(z_ref[...].astype(F32))
    mean = jnp.sum(gated * gated, axis=1, keepdims=True) * (1.0 / GWIDTH)
    out_ref[...] = (gated * lax.rsqrt(mean + EPS) * gain_ref[...]).astype(BF)


def add_incoming(piece_ref, s1_ref, gain_ref, out_ref):
    for j in range(out_ref.shape[0]):
        at = slice((j // 2) * LANES, (j // 2 + 1) * LANES)
        came = s1_ref[(j % 2) * 64 : (j % 2) * 64 + 64, at].astype(F32)
        out_ref[j] = (piece_ref[j].astype(F32) + gain_ref[0:1, at] * came).astype(BF)


def pass_on(s1_ref, entry_ref, out_ref):
    out_ref[...] = (entry_ref[8:9, :] * s1_ref[...].astype(F32)).astype(BF)


def combine(len_ref, owner_ref, got_ref, out_ref):
    row16 = lax.broadcasted_iota(I32, (16, LANES), 0)

    def one(r, carry):
        first, before = carry
        last = first + len_ref[0, r] - 1
        home = last >> 9
        second = before == home
        h1 = jnp.maximum(home - 1, 0)
        slot = owner_ref[0, r]
        extra = got_ref[home, 128:144, :].astype(F32)
        gain = jnp.where(second, 0.0, extra[0:1] + extra[1:2])
        k = pl.multiple_of(jnp.where(second, 64, 0), 64)
        own = got_ref[home, pl.ds(k, 64), :].astype(F32)
        out_ref[slot, 0:64, :] = (own + gain * got_ref[h1, 0:64, :].astype(F32)).astype(BF)
        tail = jnp.where(second, pltpu.roll(extra, 12, 0), pltpu.roll(extra, 14, 0))
        out_ref[slot, 64:80, :] = jnp.where(row16 < 2, tail, 0.0).astype(BF)
        return last + 1, home

    lax.fori_loop(0, REQS, one, (jnp.int32(0), jnp.int32(-1)), unroll=2)


def finish(got_ref, state_ref, tx_ref, tbc_ref):
    tails = [got_ref[j, 64:80, :].astype(F32) for j in range(REQS)]
    for t in range(WIDTH // LANES):
        at = slice(t * LANES, (t + 1) * LANES)
        block = jnp.concatenate(
            [got_ref[2 * t, 0:64, :], got_ref[2 * t + 1, 0:64, :]], axis=0
        ).astype(F32)
        turned = block.T
        state_ref[2 * t] = turned[0:64]
        state_ref[2 * t + 1] = turned[64:128]
        tx_ref[:, at] = jnp.concatenate([tails[2 * t][0:2], tails[2 * t + 1][0:1]], axis=0).astype(BF)
    for k in range(KW - 1):
        for q in range(4):
            value = tails[2 * (4 * k + q) + 1][1:2].astype(BF)
            tbc_ref[k, q // 2 : q // 2 + 1, (q % 2) * LANES : (q % 2 + 1) * LANES] = value


def call(kernel, grid, ins, outs, scratch=(), flops=0, nbytes=0, aliases=None, limit=None):
    return pl.pallas_call(
        kernel,
        grid=grid,
        in_specs=ins,
        out_specs=[o[1] for o in outs],
        out_shape=[o[0] for o in outs],
        scratch_shapes=list(scratch),
        input_output_aliases=aliases or {},
        compiler_params=pltpu.CompilerParams(vmem_limit_bytes=limit or LARGE),
        cost_estimate=pl.CostEstimate(flops=flops, bytes_accessed=nbytes, transcendentals=0),
    )


def whole(*shape):
    return pl.BlockSpec(shape, lambda *_: (0,) * len(shape))


def on_device(
    x_in, bc_in, z_in, dt_in, conv_x_w, conv_x_b, conv_bc_w, conv_bc_b, a_log, dt_bias, skip_d,
    norm_gain, lengths, owner_slot,
):
    x = x_in[0]
    bc = bc_in[0].reshape(TOK, BCW)
    z = z_in[0]
    index = lax.axis_index("ctx").astype(I32).reshape(1)
    smem = pl.BlockSpec(memory_space=pltpu.SMEM)
    shape = jax.ShapeDtypeStruct
    cols = lambda rows: pl.BlockSpec((rows, SW), lambda s: (0, s))
    ends = bc_in[0, TOK - HALO :].reshape(HALO, BCW)
    halo = shift_in(jnp.concatenate([x[TOK - HALO :], ends], axis=1), 1)
    halo_cols = pl.BlockSpec((HALO, BCW), lambda s: (0, WIDTH // BCW))

    vmem = pl.BlockSpec(memory_space=pltpu.VMEM)
    by_head = shape((TOK, LANES), F32)
    cum, step, fl, wst, passing = call(
        stage_p,
        (),
        [smem, vmem, vmem, vmem, vmem],
        [
            (by_head, vmem),
            (by_head, vmem),
            (shape((TOK, LANES), I32), vmem),
            (shape((TOK + 16, LANES), BF), vmem),
            (shape((16, LANES), F32), vmem),
        ],
        flops=10**8,
        nbytes=2**20,
    )(index, lengths, dt_in[0].T, a_log.reshape(1, HEADS), dt_bias.reshape(1, HEADS))

    xc, bcc, ent, left, entry = call(
        stage_a,
        (STEPS,),
        [
            cols(TOK),
            cols(HALO),
            whole(TOK, BCW),
            halo_cols,
            cols(KW),
            cols(1),
            whole(KW, 2, 2 * LANES),
            whole(2, 2 * LANES),
            whole(TOK, LANES),
            whole(TOK + 16, LANES),
        ],
        [
            (shape((TOK, WIDTH), BF), cols(TOK)),
            (shape((TOK, BCW), BF), whole(TOK, BCW)),
            (
                shape((NC, STATE, WIDTH), BF),
                pl.BlockSpec((NC, STATE, SW), lambda s: (0, 0, s)),
            ),
            (shape((STATE, WIDTH), BF), cols(STATE)),
            (shape((16, WIDTH), F32), cols(16)),
        ],
        [
            pltpu.VMEM((KW - 1, TOK, LANES), F32),
            pltpu.VMEM((TOK + 16, SW), F32),
            pltpu.VMEM((GROUPS * NC, STATE, STRETCH), BF),
        ],
        flops=10**9,
        nbytes=10 * 2**20,
    )(
        x, halo, bc, halo, conv_x_w, conv_x_b.reshape(1, WIDTH), conv_bc_w, conv_bc_b, fl, wst
    )

    s1 = shift_in(left, 1)
    crossed = shift_pairs(left, ROW_Y - 1, (ROW_Y - 2,))
    far_gain = shift_pairs(passing, 1, (ROW_Y - 1,))

    pieces, gain = call(
        stage_e,
        (STEPS,),
        [
            smem,
            smem,
            cols(TOK),
            cols(HALO),
            whole(TOK, BCW),
            halo_cols,
            cols(TOK),
            whole(TOK, BCW),
            whole(TOK, LANES),
            whole(TOK, LANES),
            pl.BlockSpec((NC, STATE, SW), lambda s: (0, 0, s)),
            cols(STATE),
        ],
        [
            (
                shape((32, PIECE, LANES), BF),
                pl.BlockSpec((2 * SLT, PIECE, LANES), lambda s: (s, 0, 0)),
            ),
            (shape((8, WIDTH), F32), cols(8)),
        ],
        [
            pltpu.VMEM((2 * STRETCH + 16, LANES), BF),
            pltpu.VMEM((2 * STRETCH + 16, SW), F32),
            pltpu.SMEM((5,), I32),
        ],
        flops=5 * 10**8,
        nbytes=8 * 2**20,
    )(index, lengths, x, halo, bc, halo, xc, bcc, cum, step, ent, left)

    by_row = lambda width: pl.BlockSpec((STRETCH, width), lambda c: (c, 0))
    (y,) = call(
        stage_b,
        (NC,),
        [by_row(WIDTH), by_row(BCW), by_row(LANES), by_row(LANES), by_row(LANES), whole(1, WIDTH)],
        [(shape((TOK, WIDTH), F32), by_row(WIDTH))],
        flops=10**9,
        nbytes=20 * 2**20,
    )(xc, bcc, cum, step, fl, jnp.repeat(skip_d, HEAD_DIM).reshape(1, WIDTH))

    s1, crossed = lax.optimization_barrier((s1, crossed))
    part = pl.BlockSpec((16, 64, LANES), lambda s: (s, 0, 0))
    half = lambda rows: pl.BlockSpec((rows, GWIDTH), lambda s: (0, s))
    (pieces,) = call(
        add_incoming,
        (2,),
        [part, half(STATE), half(8)],
        [(shape((32, PIECE, LANES), BF), part)],
        flops=10**7,
        nbytes=2 * 2**20,
        aliases={0: 0},
    )(pieces, s1, gain)
    got = lax.all_to_all(pieces, "ctx", split_axis=0, concat_axis=0, tiled=True)

    (passed,) = call(
        pass_on,
        (2,),
        [half(STATE), half(16)],
        [(shape((STATE, WIDTH), BF), half(STATE))],
        flops=10**7,
        nbytes=2 * 2**20,
        limit=SMALL,
    )(s1, entry)
    s2 = shift_pairs(passed, 1, range(ROW_Y - 1))
    count = lax.axis_size("ctx")
    far = lax.ppermute(crossed, "ctx", [(i + 1, i) for i in range(0, count, ROW_Y)])

    got, s2, far, far_gain, y = lax.optimization_barrier((got, s2, far, far_gain, y))
    (back,) = call(
        combine,
        (),
        [smem, smem, pl.BlockSpec(memory_space=pltpu.VMEM)],
        [(shape((REQS, BACK, LANES), BF), pl.BlockSpec(memory_space=pltpu.VMEM))],
        flops=10**7,
        nbytes=3 * 2**20,
        limit=SMALL,
    )(lengths, owner_slot, got)
    own = lax.all_to_all(back, "ctx", split_axis=0, concat_axis=0, tiled=True)

    back, y = lax.optimization_barrier((back, y))
    by_c = lambda g, c: (c, 0)
    by_g = lambda g, c: (0, g)
    by_cg = lambda g, c: (c, g)
    (mixed,) = call(
        stage_c,
        (GROUPS, NC),
        [
            pl.BlockSpec((STRETCH, GWIDTH), by_cg),
            pl.BlockSpec((STRETCH, GWIDTH), by_cg),
            pl.BlockSpec((STRETCH, LANES), lambda g, c: (c, GROUPS + g)),
            pl.BlockSpec((1, STATE, GWIDTH), lambda g, c: (c, 0, g)),
            pl.BlockSpec((STATE, GWIDTH), by_g),
            pl.BlockSpec((STATE, GWIDTH), by_g),
            pl.BlockSpec((STATE, GWIDTH), by_g),
            whole(16, LANES),
            pl.BlockSpec((16, GWIDTH), by_g),
            pl.BlockSpec((STRETCH, LANES), by_c),
            pl.BlockSpec((STRETCH, LANES), by_c),
            pl.BlockSpec((1, GWIDTH), by_g),
        ],
        [(shape((TOK, WIDTH), BF), pl.BlockSpec((STRETCH, GWIDTH), by_cg))],
        flops=10**9,
        nbytes=15 * 2**20,
    )(y, z, bcc, ent, s1, s2, far, far_gain, entry, cum, fl, norm_gain.reshape(1, WIDTH))

    own, mixed = lax.optimization_barrier((own, mixed))
    swapped = lax.ppermute(own, "side", [(0, 1), (1, 0)])
    state, tail_x, tail_bc = call(
        finish,
        (),
        [pl.BlockSpec(memory_space=pltpu.VMEM)],
        [
            (shape((HEADS, HEAD_DIM, STATE), F32), pl.BlockSpec(memory_space=pltpu.VMEM)),
            (shape((KW - 1, WIDTH), BF), pl.BlockSpec(memory_space=pltpu.VMEM)),
            (shape((KW - 1, 2, 2 * LANES), BF), pl.BlockSpec(memory_space=pltpu.VMEM)),
        ],
        flops=10**7,
        nbytes=3 * 2**20,
        limit=SMALL,
    )(swapped)
    return mixed[None], state[None, None], tail_x[None, None], tail_bc[None, None]


def solution(mesh):
    placed = (
        P("side", "ctx", "head"),
        P("side", "ctx", None, "head"),
        P("side", "ctx", "head"),
        P("side", "ctx", "head"),
        P(None, "head"),
        P("head"),
        P(None, None, "head"),
        P(None, "head"),
        P("head"),
        P("head"),
        P("head"),
        P("head"),
        P("side", None),
        P("side", None),
    )
    return jax.shard_map(
        on_device,
        mesh=mesh,
        in_specs=placed,
        out_specs=(
            P("side", "ctx", "head"),
            P("side", "ctx", "head", None, None),
            P("side", "ctx", None, "head"),
            P("side", "ctx", None, None, "head"),
        ),
        check_vma=False,
    )
```

```python
import jax
import jax.numpy as jnp
from jax import lax
from jax.experimental import pallas as pl
from jax.experimental.pallas import tpu as pltpu
from jax.sharding import PartitionSpec as P

HEAD_DIM = 64
STATE = 128
STRETCH = 128
LANES = 128
HALO = 16
KW = 4
EPS = 1e-05
BF = jnp.bfloat16
F32 = jnp.float32
I32 = jnp.int32
LARGE = 60 * 1024 * 1024
SMALL = 16 * 1024 * 1024

TOK = 512
NC = TOK // STRETCH
WIDTH = 2048
HEADS = WIDTH // HEAD_DIM
GROUPS = 2
GWIDTH = WIDTH // GROUPS
BCW = 512
REQS = 32
ROW_Y = 4
STEPS = 4
SW = WIDTH // STEPS
SLT = SW // LANES
PIECE = 2 * 64 + 8
BACK = 64 + 8


def shift_in(block, distance):
    count = lax.axis_size("ctx")
    return lax.ppermute(block, "ctx", [(i, i + distance) for i in range(count - distance)])


def shift_pairs(block, distance, keep):
    count = lax.axis_size("ctx")
    pairs = [(i, i + distance) for i in range(count - distance) if i % ROW_Y in keep]
    return lax.ppermute(block, "ctx", pairs)


def swish(v):
    half = 0.5 * v
    return half + half * jnp.tanh(half)


def split3(v, lane):
    hi = v.astype(BF).astype(F32)
    rest = v - hi
    mid = rest.astype(BF).astype(F32)
    low = rest - mid
    return jnp.where(
        lane < HEADS, hi, jnp.where(lane < 2 * HEADS, mid, jnp.where(lane < 3 * HEADS, low, 0.0))
    ).astype(BF)


def spread_matrix(first_head, width):
    row = lax.broadcasted_iota(I32, (LANES, width), 0)
    col = lax.broadcasted_iota(I32, (LANES, width), 1)
    same = ((row & (HEADS - 1)) == (col >> 6) + first_head) & (row < 3 * HEADS)
    return jnp.where(same, 1.0, 0.0).astype(BF)


def conv_tile(ext, taps, bias, masks):
    acc = bias + taps[KW - 1] * ext[HALO:]
    for d in range(1, KW):
        acc = acc + taps[KW - 1 - d] * (pltpu.roll(ext, d, 0)[HALO:] * masks[d - 1])
    return swish(acc)


def scan_lengths(idx_ref, len_ref):
    zero = jnp.int32(0)

    def scan(r, carry):
        first, count, behind, e0, f0, e1, f1, fa = carry
        last = first + len_ref[0, r] - 1
        ends = (last >= 0) & (last < TOK)
        take0, take1 = ends & (count == 0), ends & (count == 1)
        points = [c * STRETCH + STRETCH - 1 for c in range(NC)]
        fa = tuple(
            jnp.where((first <= p) & (last >= p), first, old) for p, old in zip(points, fa)
        )
        return (
            last + 1,
            count + jnp.where(ends, 1, 0),
            behind + jnp.where((last >= -TOK) & (last < 0), 1, 0),
            jnp.where(take0, last, e0),
            jnp.where(take0, first, f0),
            jnp.where(take1, last, e1),
            jnp.where(take1, first, f1),
            fa,
        )

    start = -idx_ref[0] * TOK
    out = lax.fori_loop(
        0, REQS, scan, (start, zero, zero, zero, zero, zero, zero, (zero,) * NC), unroll=4
    )
    return out[1:]


def stretch_gains(cum_ref, fa):
    through = []
    gains = [jnp.ones((1, LANES), F32)]
    for c in range(NC):
        end = cum_ref[(c + 1) * STRETCH - 1 : (c + 1) * STRETCH, :]
        through.append(jnp.where(fa[c] < c * STRETCH, jnp.exp(end), 0.0))
        gains.append(gains[-1] * through[-1])
    return through, gains


def as_rows(values):
    row16 = lax.broadcasted_iota(I32, (16, LANES), 0)
    block = jnp.zeros((16, LANES), F32)
    for i, v in enumerate(values):
        block = jnp.where(row16 == i, v, block)
    return block


def stage_p(
    idx_ref, len_ref, dt_ref, al_ref, db_ref, cum_ref, step_ref, fl_ref, wst_ref, pass_ref
):
    lane = lax.broadcasted_iota(I32, (STRETCH, LANES), 1)
    row = lax.broadcasted_iota(I32, (STRETCH, LANES), 0)
    lane_f = lane.astype(F32)
    start = (-idx_ref[0] * TOK).astype(F32)
    lengths = jnp.concatenate([len_ref[...].astype(F32)] * 4, axis=1)
    earlier = jnp.where((row < lane) & (row < REQS), 1.0, 0.0)
    first = start + jnp.dot(
        jnp.broadcast_to(lengths, (8, LANES)),
        earlier,
        precision=lax.Precision.HIGHEST,
        preferred_element_type=F32,
    )[0:1, :]
    first = jnp.where(lane_f[0:1, :] < REQS, first, start)
    coef = -jnp.exp(jnp.concatenate([al_ref[...]] * 4, axis=1))
    bias = jnp.concatenate([db_ref[...]] * 4, axis=1)
    lower = jnp.where(row >= lane, 1.0, 0.0)
    through = []
    gains = [jnp.ones((1, LANES), F32)]
    for c in range(NC):
        rows = slice(c * STRETCH, (c + 1) * STRETCH)
        here = row + c * STRETCH
        started = jnp.where(first <= here.astype(F32), first, start)
        fl = jnp.broadcast_to(jnp.max(started, axis=1, keepdims=True), (STRETCH, LANES))
        fl = fl.astype(I32)
        fl_ref[rows, :] = fl
        raw = jnp.concatenate([dt_ref[:, rows]] * 4, axis=0).T + bias
        step = jnp.maximum(raw, 0.0) + jnp.log1p(jnp.exp(-jnp.abs(raw)))
        step_ref[rows, :] = step
        cum = jnp.dot(
            lower, coef * step, precision=lax.Precision.HIGHEST, preferred_element_type=F32
        )
        cum_ref[rows, :] = cum
        end, fa = cum[STRETCH - 1 :, :], fl[STRETCH - 1 :, :]
        w = jnp.exp(end - cum) * step
        wst_ref[rows, :] = split3(jnp.where(here >= fa, w, 0.0), lane)
        through.append(jnp.where(fa < c * STRETCH, jnp.exp(end), 0.0))
        gains.append(gains[-1] * through[-1])
    lane16 = lax.broadcasted_iota(I32, (16, LANES), 1)
    wst_ref[NC * STRETCH :, :] = split3(as_rows(through + gains), lane16)
    pass_ref[...] = jnp.broadcast_to(gains[NC], (16, LANES))


def stage_a(
    x_ref, xh_ref, bc_ref, bch_ref, wx_ref, bx_ref, wbc_ref, bbc_ref, fl_ref, wst_ref,
    xc_ref, bcc_ref, ent_ref, s_ref, entry_ref,
    mask_scr, spread_scr, bt_scr,
):
    s = pl.program_id(0)
    row = lax.broadcasted_iota(I32, (STRETCH, LANES), 0)

    @pl.when(s == 0)
    def _():
        for c in range(NC):
            rows = slice(c * STRETCH, (c + 1) * STRETCH)
            since = row + c * STRETCH - fl_ref[rows, :]
            for d in range(1, KW):
                mask_scr[d - 1, rows, :] = jnp.where(since >= d, 1.0, 0.0)
        for part in range(1):
            for g in range(GROUPS):
                at = slice((part * GROUPS + g) * LANES, (part * GROUPS + g + 1) * LANES)
                own = slice(g * LANES, (g + 1) * LANES)
                taps = [wbc_ref[k, part : part + 1, own] for k in range(KW)]
                off = bbc_ref[part : part + 1, own]
                for c in range(NC):
                    if c == 0:
                        ext = jnp.concatenate([bch_ref[:, at], bc_ref[0:STRETCH, at]], axis=0)
                    else:
                        ext = bc_ref[c * STRETCH - HALO : (c + 1) * STRETCH, at]
                    rows = slice(c * STRETCH, (c + 1) * STRETCH)
                    masks = [mask_scr[d, rows, :] for d in range(KW - 1)]
                    out = conv_tile(ext.astype(F32), taps, off, masks).astype(BF)
                    bcc_ref[rows, at] = out
                    if part == 0:
                        bt_scr[g * NC + c] = out.astype(F32).T.astype(BF)

    spread_scr[...] = jnp.dot(
        wst_ref[...], spread_matrix(s * (SW // HEAD_DIM), SW), preferred_element_type=F32
    )
    ex = NC * STRETCH
    group = s // (STEPS // GROUPS)
    entry_ref[...] = spread_scr[ex:, :]
    entering = None
    for c in range(NC):
        rows = slice(c * STRETCH, (c + 1) * STRETCH)
        masks = [mask_scr[d, rows, :] for d in range(KW - 1)]
        scaled = []
        for t in range(SLT):
            at = slice(t * LANES, (t + 1) * LANES)
            if c == 0:
                ext = jnp.concatenate([xh_ref[:, at], x_ref[0:STRETCH, at]], axis=0)
            else:
                ext = x_ref[c * STRETCH - HALO : (c + 1) * STRETCH, at]
            taps = [wx_ref[k : k + 1, at] for k in range(KW)]
            out = conv_tile(ext.astype(F32), taps, bx_ref[:, at], masks).astype(BF)
            xc_ref[rows, at] = out
            scaled.append((out.astype(F32) * spread_scr[rows, at]).astype(BF))
        local = jnp.dot(
            bt_scr[group * NC + c], jnp.concatenate(scaled, axis=1), preferred_element_type=F32
        )
        if c == 0:
            ent_ref[0] = jnp.zeros((STATE, SW), BF)
            entering = local
        else:
            ent_ref[c] = entering.astype(BF)
            entering = spread_scr[ex + c : ex + c + 1, :] * entering + local
    s_ref[...] = entering.astype(BF)


def stage_e(
    idx_ref, len_ref, x_ref, xh_ref, bc_ref, bch_ref, xc_ref, bcc_ref, cum_ref, step_ref, ent_ref,
    s_ref, wbc_ref, bbc_ref, fl_ref,
    piece_ref, gain_ref, cc_ref,
    wst_scr, spread_scr, sc_scr,
):
    s = pl.program_id(0)
    lane = lax.broadcasted_iota(I32, (STRETCH, LANES), 1)
    row = lax.broadcasted_iota(I32, (STRETCH, LANES), 0)
    ex = 2 * STRETCH

    @pl.when(s == 0)
    def _():
        for c in range(NC):
            rows = slice(c * STRETCH, (c + 1) * STRETCH)
            since = row + c * STRETCH - fl_ref[rows, :]
            masks = [jnp.where(since >= d, 1.0, 0.0) for d in range(1, KW)]
            for g in range(GROUPS):
                own = slice(g * LANES, (g + 1) * LANES)
                at = slice((GROUPS + g) * LANES, (GROUPS + g + 1) * LANES)
                if c == 0:
                    ext = jnp.concatenate([bch_ref[:, at], bc_ref[0:STRETCH, at]], axis=0)
                else:
                    ext = bc_ref[c * STRETCH - HALO : (c + 1) * STRETCH, at]
                taps = [wbc_ref[k, 1:2, own] for k in range(KW)]
                cc_ref[rows, own] = conv_tile(
                    ext.astype(F32), taps, bbc_ref[1:2, own], masks
                ).astype(BF)
        count, behind, e0, f0, e1, f1, fa = scan_lengths(idx_ref, len_ref)
        sc_scr[0], sc_scr[1], sc_scr[2], sc_scr[3], sc_scr[4] = e0, f0, e1, f1, count
        inflow = []
        for k, (e, f) in enumerate(((e0, f0), (e1, f1))):
            base = pl.multiple_of((e >> 7) * STRETCH, STRETCH)
            here = row + base
            end = cum_ref[pl.ds(e, 1), :]
            w = jnp.exp(end - cum_ref[pl.ds(base, STRETCH), :]) * step_ref[pl.ds(base, STRETCH), :]
            w = jnp.where((here >= f) & (here <= e), w, 0.0)
            wst_scr[k * STRETCH : (k + 1) * STRETCH, :] = split3(w, lane)
            inflow.append(jnp.where(f < base, jnp.exp(end), 0.0))
        _, gains = stretch_gains(cum_ref, fa)
        gain = gains[0]
        for c in range(1, NC):
            gain = jnp.where((e0 >> 7) == c, gains[c], gain)
        gain = gain * inflow[0]
        by_owner = jnp.where((count > 0) & (behind == 0), gain, 0.0)
        by_sender = jnp.where(count == 0, gains[NC], jnp.where(behind == 0, 0.0, gain))
        lane16 = lax.broadcasted_iota(I32, (16, LANES), 1)
        wst_scr[ex:, :] = split3(as_rows(inflow + [by_owner, by_sender]), lane16)

    e0, f0, e1, f1 = sc_scr[0], sc_scr[1], sc_scr[2], sc_scr[3]
    spread_scr[...] = jnp.dot(
        wst_scr[...], spread_matrix(s * (SW // HEAD_DIM), SW), preferred_element_type=F32
    )
    gain_ref[...] = jnp.broadcast_to(spread_scr[ex + 3 : ex + 4, :], (8, SW))
    group = s // (STEPS // GROUPS)
    for k, e in enumerate((e0, e1)):
        c = e >> 7
        base = pl.multiple_of(c * STRETCH, STRETCH)
        at = k * STRETCH
        scaled = (
            xc_ref[pl.ds(base, STRETCH), :].astype(F32) * spread_scr[at : at + STRETCH, :]
        ).astype(BF)
        b = jnp.where(
            group == 0,
            bcc_ref[pl.ds(base, STRETCH), 0:LANES].astype(F32),
            bcc_ref[pl.ds(base, STRETCH), LANES : 2 * LANES].astype(F32),
        )
        final = spread_scr[ex + k : ex + k + 1, :] * ent_ref[c].astype(F32) + jnp.dot(
            b.T.astype(BF), scaled, preferred_element_type=F32
        )
        if k == 0:
            final = jnp.where(sc_scr[4] == 0, s_ref[...].astype(F32), final)
        final = final.astype(BF)
        for j in range(2 * SLT):
            piece_ref[j, k * 64 : k * 64 + 64, :] = final[
                (j % 2) * 64 : (j % 2) * 64 + 64, (j // 2) * LANES : (j // 2 + 1) * LANES
            ]

    tails_x, tails_bc = [], []
    pick_row = lax.broadcasted_iota(I32, (16, 2 * HALO), 0)
    pick_col = lax.broadcasted_iota(I32, (16, 2 * HALO), 1)
    for e, f in ((e0, f0), (e1, f1)):
        base = pl.multiple_of((e >> 4) * HALO, HALO)
        before = pl.multiple_of(jnp.maximum(base - HALO, 0), HALO)
        source = e - (KW - 2) + pick_row
        pick = (pick_col + base - HALO == source) & (source >= f) & (pick_row < KW - 1)
        pick = jnp.where(pick, 1.0, 0.0).astype(BF)

        def tail(ref, halo_ref):
            head = jnp.where(base > 0, ref[pl.ds(before, HALO), :], halo_ref[...])
            window = jnp.concatenate([head, ref[pl.ds(base, HALO), :]], axis=0)
            return jnp.dot(pick, window, preferred_element_type=F32)

        tails_x.append(tail(x_ref, xh_ref))
        tails_bc.append(tail(bc_ref, bch_ref))
    row16 = lax.broadcasted_iota(I32, (16, LANES), 0)
    for t in range(SLT):
        at = slice(t * LANES, (t + 1) * LANES)
        gain = spread_scr[ex + 2 : ex + 3, at]
        gain_hi = gain.astype(BF).astype(F32)
        bc_rows = []
        for k in range(2):
            one = tails_bc[k][:, at]
            bc_rows.append(jnp.sum(jnp.where(row16 == s, one, 0.0), axis=0, keepdims=True))
        for half in range(2):
            values = [gain_hi, gain - gain_hi]
            for k in range(2):
                one = tails_x[k][:, at]
                values += [one[0:1], one[1:2]] if half == 0 else [one[2:3], bc_rows[k]]
            piece_ref[2 * t + half, 128:136, :] = as_rows(values)[0:8].astype(BF)


def stage_b(xc_ref, bcc_ref, cc_ref, cum_ref, step_ref, fl_ref, skip_ref, y_ref):
    c = pl.program_id(0)
    row = lax.broadcasted_iota(I32, (STRETCH, LANES), 0)
    lane = lax.broadcasted_iota(I32, (STRETCH, LANES), 1)
    keep = (lane <= row) & (lane + c * STRETCH >= fl_ref[...])
    cum = cum_ref[...]
    cum_t = cum.T
    step_t = step_ref[...].T
    low = lax.broadcasted_iota(I32, (STRETCH, LANES), 1) < HEAD_DIM
    for g in range(GROUPS):
        b = bcc_ref[:, g * LANES : (g + 1) * LANES]
        cc = cc_ref[:, g * LANES : (g + 1) * LANES]
        scores = lax.dot_general(cc, b, (((1,), (1,)), ((), ())), preferred_element_type=F32)
        for i in range(HEADS // GROUPS // 2):
            pair = g * (HEADS // GROUPS // 2) + i
            weights = []
            for h in (2 * pair, 2 * pair + 1):
                decay = jnp.exp(jnp.where(keep, cum[:, h : h + 1] - cum_t[h : h + 1, :], -jnp.inf))
                weights.append((scores * (decay * step_t[h : h + 1, :])).astype(BF))
            at = slice(pair * LANES, (pair + 1) * LANES)
            x = xc_ref[:, at]
            xf = x.astype(F32)
            both = jnp.concatenate(
                [jnp.where(low, xf, 0.0).astype(BF), jnp.where(low, 0.0, xf).astype(BF)], axis=0
            )
            inner = jnp.dot(
                jnp.concatenate(weights, axis=1), both, preferred_element_type=F32
            )
            y_ref[:, at] = inner + skip_ref[:, at] * xf


def stage_c(
    y_ref, z_ref, c_ref, ent_ref, s1_ref, s2_ref, far_ref, far_gain_ref, entry_ref, cum_ref, fl_ref, gain_ref, out_ref
):
    g, c = pl.program_id(0), pl.program_id(1)
    lane = lax.broadcasted_iota(I32, (STRETCH, LANES), 1)
    inflow = jnp.where(fl_ref[...] < c * STRETCH, jnp.exp(cum_ref[...]), 0.0)
    both = jnp.concatenate([split3(inflow, lane), split3(far_gain_ref[...], lane[0:16])], axis=0)
    wide = jnp.dot(
        both, spread_matrix(g * (HEADS // GROUPS), GWIDTH), preferred_element_type=F32
    )
    far_gain = wide[STRETCH : STRETCH + 1, :]
    wide = wide[0:STRETCH, :]
    incoming = s1_ref[...].astype(F32) + s2_ref[...].astype(F32)
    incoming = incoming + far_gain * far_ref[...].astype(F32)
    entering = ent_ref[0].astype(F32) + entry_ref[pl.ds(NC + c, 1), :] * incoming
    carried = jnp.dot(c_ref[...], entering.astype(BF), preferred_element_type=F32)
    gated = (y_ref[...] + wide * carried) * swish(z_ref[...].astype(F32))
    mean = jnp.sum(gated * gated, axis=1, keepdims=True) * (1.0 / GWIDTH)
    out_ref[...] = (gated * lax.rsqrt(mean + EPS) * gain_ref[...]).astype(BF)


def add_incoming(piece_ref, s1_ref, gain_ref, out_ref):
    for j in range(out_ref.shape[0]):
        at = slice((j // 2) * LANES, (j // 2 + 1) * LANES)
        came = s1_ref[(j % 2) * 64 : (j % 2) * 64 + 64, at].astype(F32)
        out_ref[j] = (piece_ref[j].astype(F32) + gain_ref[0:1, at] * came).astype(BF)


def pass_on(s1_ref, entry_ref, out_ref):
    out_ref[...] = (entry_ref[8:9, :] * s1_ref[...].astype(F32)).astype(BF)


def combine(len_ref, owner_ref, got_ref, out_ref):
    row8 = lax.broadcasted_iota(I32, (8, LANES), 0)

    def one(r, carry):
        first, before = carry
        last = first + len_ref[0, r] - 1
        home = last >> 9
        second = before == home
        h1 = jnp.maximum(home - 1, 0)
        slot = owner_ref[0, r]
        extra = got_ref[home, 128:136, :].astype(F32)
        gain = jnp.where(second, 0.0, extra[0:1] + extra[1:2])
        k = pl.multiple_of(jnp.where(second, 64, 0), 64)
        own = got_ref[home, pl.ds(k, 64), :].astype(F32)
        out_ref[slot, 0:64, :] = (own + gain * got_ref[h1, 0:64, :].astype(F32)).astype(BF)
        tail = jnp.where(second, pltpu.roll(extra, 4, 0), pltpu.roll(extra, 6, 0))
        out_ref[slot, 64:72, :] = jnp.where(row8 < 2, tail, 0.0).astype(BF)
        return last + 1, home

    lax.fori_loop(0, REQS, one, (jnp.int32(0), jnp.int32(-1)), unroll=2)


def finish(got_ref, state_ref, tx_ref, tbc_ref):
    tails = [got_ref[j, 64:72, :].astype(F32) for j in range(REQS)]
    for t in range(WIDTH // LANES):
        at = slice(t * LANES, (t + 1) * LANES)
        block = jnp.concatenate(
            [got_ref[2 * t, 0:64, :], got_ref[2 * t + 1, 0:64, :]], axis=0
        ).astype(F32)
        turned = block.T
        state_ref[2 * t] = turned[0:64]
        state_ref[2 * t + 1] = turned[64:128]
        tx_ref[:, at] = jnp.concatenate([tails[2 * t][0:2], tails[2 * t + 1][0:1]], axis=0).astype(BF)
    for k in range(KW - 1):
        for q in range(4):
            value = tails[2 * (4 * k + q) + 1][1:2].astype(BF)
            tbc_ref[k, q // 2 : q // 2 + 1, (q % 2) * LANES : (q % 2 + 1) * LANES] = value


def call(kernel, grid, ins, outs, scratch=(), flops=0, nbytes=0, aliases=None, limit=None):
    return pl.pallas_call(
        kernel,
        grid=grid,
        in_specs=ins,
        out_specs=[o[1] for o in outs],
        out_shape=[o[0] for o in outs],
        scratch_shapes=list(scratch),
        input_output_aliases=aliases or {},
        compiler_params=pltpu.CompilerParams(vmem_limit_bytes=limit or LARGE),
        cost_estimate=pl.CostEstimate(flops=flops, bytes_accessed=nbytes, transcendentals=0),
    )


def whole(*shape):
    return pl.BlockSpec(shape, lambda *_: (0,) * len(shape))


def on_device(
    x_in, bc_in, z_in, dt_in, conv_x_w, conv_x_b, conv_bc_w, conv_bc_b, a_log, dt_bias, skip_d,
    norm_gain, lengths, owner_slot,
):
    x = x_in[0]
    bc = bc_in[0].reshape(TOK, BCW)
    z = z_in[0]
    index = lax.axis_index("ctx").astype(I32).reshape(1)
    smem = pl.BlockSpec(memory_space=pltpu.SMEM)
    shape = jax.ShapeDtypeStruct
    cols = lambda rows: pl.BlockSpec((rows, SW), lambda s: (0, s))
    ends = bc_in[0, TOK - HALO :].reshape(HALO, BCW)
    halo = shift_in(jnp.concatenate([x[TOK - HALO :], ends], axis=1), 1)
    halo_cols = pl.BlockSpec((HALO, BCW), lambda s: (0, WIDTH // BCW))

    vmem = pl.BlockSpec(memory_space=pltpu.VMEM)
    by_head = shape((TOK, LANES), F32)
    cum, step, fl, wst, passing = call(
        stage_p,
        (),
        [smem, vmem, vmem, vmem, vmem],
        [
            (by_head, vmem),
            (by_head, vmem),
            (shape((TOK, LANES), I32), vmem),
            (shape((TOK + 16, LANES), BF), vmem),
            (shape((16, LANES), F32), vmem),
        ],
        flops=10**8,
        nbytes=2**20,
    )(index, lengths, dt_in[0].T, a_log.reshape(1, HEADS), dt_bias.reshape(1, HEADS))

    xc, bcc, ent, left, entry = call(
        stage_a,
        (STEPS,),
        [
            cols(TOK),
            cols(HALO),
            whole(TOK, BCW),
            halo_cols,
            cols(KW),
            cols(1),
            whole(KW, 2, 2 * LANES),
            whole(2, 2 * LANES),
            whole(TOK, LANES),
            whole(TOK + 16, LANES),
        ],
        [
            (shape((TOK, WIDTH), BF), cols(TOK)),
            (shape((TOK, GROUPS * LANES), BF), whole(TOK, GROUPS * LANES)),
            (
                shape((NC, STATE, WIDTH), BF),
                pl.BlockSpec((NC, STATE, SW), lambda s: (0, 0, s)),
            ),
            (shape((STATE, WIDTH), BF), cols(STATE)),
            (shape((16, WIDTH), F32), cols(16)),
        ],
        [
            pltpu.VMEM((KW - 1, TOK, LANES), F32),
            pltpu.VMEM((TOK + 16, SW), F32),
            pltpu.VMEM((GROUPS * NC, STATE, STRETCH), BF),
        ],
        flops=10**9,
        nbytes=10 * 2**20,
    )(
        x, halo, bc, halo, conv_x_w, conv_x_b.reshape(1, WIDTH), conv_bc_w, conv_bc_b, fl, wst
    )

    s1 = shift_in(left, 1)
    crossed = shift_pairs(left, ROW_Y - 1, (ROW_Y - 2,))
    far_gain = shift_pairs(passing, 1, (ROW_Y - 1,))

    pieces, gain, cc = call(
        stage_e,
        (STEPS,),
        [
            smem,
            smem,
            cols(TOK),
            cols(HALO),
            whole(TOK, BCW),
            halo_cols,
            cols(TOK),
            whole(TOK, GROUPS * LANES),
            whole(TOK, LANES),
            whole(TOK, LANES),
            pl.BlockSpec((NC, STATE, SW), lambda s: (0, 0, s)),
            cols(STATE),
            whole(KW, 2, 2 * LANES),
            whole(2, 2 * LANES),
            whole(TOK, LANES),
        ],
        [
            (
                shape((32, PIECE, LANES), BF),
                pl.BlockSpec((2 * SLT, PIECE, LANES), lambda s: (s, 0, 0)),
            ),
            (shape((8, WIDTH), F32), cols(8)),
            (shape((TOK, GROUPS * LANES), BF), whole(TOK, GROUPS * LANES)),
        ],
        [
            pltpu.VMEM((2 * STRETCH + 16, LANES), BF),
            pltpu.VMEM((2 * STRETCH + 16, SW), F32),
            pltpu.SMEM((5,), I32),
        ],
        flops=5 * 10**8,
        nbytes=8 * 2**20,
    )(index, lengths, x, halo, bc, halo, xc, bcc, cum, step, ent, left, conv_bc_w, conv_bc_b, fl)

    by_row = lambda width: pl.BlockSpec((STRETCH, width), lambda c: (c, 0))
    (y,) = call(
        stage_b,
        (NC,),
        [by_row(WIDTH), by_row(GROUPS * LANES), by_row(GROUPS * LANES), by_row(LANES), by_row(LANES), by_row(LANES), whole(1, WIDTH)],
        [(shape((TOK, WIDTH), F32), by_row(WIDTH))],
        flops=10**9,
        nbytes=20 * 2**20,
    )(xc, bcc, cc, cum, step, fl, jnp.repeat(skip_d, HEAD_DIM).reshape(1, WIDTH))

    s1, crossed = lax.optimization_barrier((s1, crossed))
    part = pl.BlockSpec((16, 64, LANES), lambda s: (s, 0, 0))
    half = lambda rows: pl.BlockSpec((rows, GWIDTH), lambda s: (0, s))
    (pieces,) = call(
        add_incoming,
        (2,),
        [part, half(STATE), half(8)],
        [(shape((32, PIECE, LANES), BF), part)],
        flops=10**7,
        nbytes=2 * 2**20,
        aliases={0: 0},
    )(pieces, s1, gain)
    got = lax.all_to_all(pieces, "ctx", split_axis=0, concat_axis=0, tiled=True)

    (passed,) = call(
        pass_on,
        (2,),
        [half(STATE), half(16)],
        [(shape((STATE, WIDTH), BF), half(STATE))],
        flops=10**7,
        nbytes=2 * 2**20,
        limit=SMALL,
    )(s1, entry)
    s2 = shift_pairs(passed, 1, range(ROW_Y - 1))
    count = lax.axis_size("ctx")
    far = lax.ppermute(crossed, "ctx", [(i + 1, i) for i in range(0, count, ROW_Y)])

    got, s2, far, far_gain, y = lax.optimization_barrier((got, s2, far, far_gain, y))
    (back,) = call(
        combine,
        (),
        [smem, smem, pl.BlockSpec(memory_space=pltpu.VMEM)],
        [(shape((REQS, BACK, LANES), BF), pl.BlockSpec(memory_space=pltpu.VMEM))],
        flops=10**7,
        nbytes=3 * 2**20,
        limit=SMALL,
    )(lengths, owner_slot, got)
    own = lax.all_to_all(back, "ctx", split_axis=0, concat_axis=0, tiled=True)

    back, y = lax.optimization_barrier((back, y))
    by_c = lambda g, c: (c, 0)
    by_g = lambda g, c: (0, g)
    by_cg = lambda g, c: (c, g)
    (mixed,) = call(
        stage_c,
        (GROUPS, NC),
        [
            pl.BlockSpec((STRETCH, GWIDTH), by_cg),
            pl.BlockSpec((STRETCH, GWIDTH), by_cg),
            pl.BlockSpec((STRETCH, LANES), lambda g, c: (c, g)),
            pl.BlockSpec((1, STATE, GWIDTH), lambda g, c: (c, 0, g)),
            pl.BlockSpec((STATE, GWIDTH), by_g),
            pl.BlockSpec((STATE, GWIDTH), by_g),
            pl.BlockSpec((STATE, GWIDTH), by_g),
            whole(16, LANES),
            pl.BlockSpec((16, GWIDTH), by_g),
            pl.BlockSpec((STRETCH, LANES), by_c),
            pl.BlockSpec((STRETCH, LANES), by_c),
            pl.BlockSpec((1, GWIDTH), by_g),
        ],
        [(shape((TOK, WIDTH), BF), pl.BlockSpec((STRETCH, GWIDTH), by_cg))],
        flops=10**9,
        nbytes=15 * 2**20,
    )(y, z, cc, ent, s1, s2, far, far_gain, entry, cum, fl, norm_gain.reshape(1, WIDTH))

    own, mixed = lax.optimization_barrier((own, mixed))
    swapped = lax.ppermute(own, "side", [(0, 1), (1, 0)])
    state, tail_x, tail_bc = call(
        finish,
        (),
        [pl.BlockSpec(memory_space=pltpu.VMEM)],
        [
            (shape((HEADS, HEAD_DIM, STATE), F32), pl.BlockSpec(memory_space=pltpu.VMEM)),
            (shape((KW - 1, WIDTH), BF), pl.BlockSpec(memory_space=pltpu.VMEM)),
            (shape((KW - 1, 2, 2 * LANES), BF), pl.BlockSpec(memory_space=pltpu.VMEM)),
        ],
        flops=10**7,
        nbytes=3 * 2**20,
        limit=SMALL,
    )(swapped)
    return mixed[None], state[None, None], tail_x[None, None], tail_bc[None, None]


def solution(mesh):
    placed = (
        P("side", "ctx", "head"),
        P("side", "ctx", None, "head"),
        P("side", "ctx", "head"),
        P("side", "ctx", "head"),
        P(None, "head"),
        P("head"),
        P(None, None, "head"),
        P(None, "head"),
        P("head"),
        P("head"),
        P("head"),
        P("head"),
        P("side", None),
        P("side", None),
    )
    return jax.shard_map(
        on_device,
        mesh=mesh,
        in_specs=placed,
        out_specs=(
            P("side", "ctx", "head"),
            P("side", "ctx", "head", None, None),
            P("side", "ctx", None, "head"),
            P("side", "ctx", None, None, "head"),
        ),
        check_vma=False,
    )
```
